32 devices in a mesh: rep: 2 (over x), ctx: 8 (over z, y), tp: 2 (over core).
Axes of the slice: x: 2, y: 2, z: 4, core: 2. Of those that a mesh axis runs over, the one named last changes fastest.
Arguments:
- queries: bfloat16 [4096, 4096], P(('rep', 'ctx'), 'tp'), parts along dimension 0, may hold values from -8 to 8
- rotated_key_rows: bfloat16 [4096, 512], P(('rep', 'ctx'), 'tp'), parts along dimension 0, may hold values from -8 to 8
- ordered_value_rows: bfloat16 [4096, 512], P(('rep', 'ctx'), 'tp'), parts along dimension 0, may hold values from -6 to 6
- block_order: int32 [32], P('rep'), parts along dimension 0, may hold values from 0 to 15, each once
- live_blocks: int32 [32, 12], P('rep'), parts along dimension 0, may hold values from -1 to 15, as said below
Outputs:
- attended: bfloat16 [4096, 4096], P(('rep', 'ctx', 'tp')), parts along dimension 0
- log_norm: float32 [64, 2048], P(('rep', 'tp'), 'ctx'), parts along dimension 0
The draws below stay inside these ranges and needn't reach their ends.
There are 2 independent parts, one for each index of `rep`. The reference program is written for one: setup_inputs(seed, part) draws one part's arguments, and reference() takes and returns one part's arrays. A program takes and returns all parts, laid end to end along the dimension named above; each array names one. Nothing has to cross between parts.
Inputs may be any that keep to these rules, and one draw needn't show every extreme that they name: `live_blocks`: row s names block s in its first slot, then distinct blocks before s, then -1 in every unused slot; row 15 fills all 12 slots.
All inputs are finite; a program needn't handle non-finite values.
Results may differ from the reference program's by a relative error of at most 0.008.
Values may be sent and summed in bfloat16 or wider, within the bound.
No kernel may reach another device: no remote copies, remote signals or barrier semaphores. Data moves between devices by JAX's collectives and lax.ppermute only.
A program may use at most 128 MiB of HBM per device.

```python
import jax
import jax.numpy as jnp
from jax import lax

QUERY_HEADS = 32
KEY_VALUE_HEADS = 4
HEAD_SIZE = 128
BLOCK_TOKENS = 128
PROMPT_TOKENS = 2048
PROMPT_BLOCKS = 16
LIVE = 12


def base_random_field(key, shape):
    return jnp.clip(jax.random.normal(key, shape, jnp.float32), -8.0, 8.0)


def draw_queries(key, part):
    sampled_field = base_random_field(jax.random.fold_in(key, 1), (PROMPT_TOKENS, QUERY_HEADS * HEAD_SIZE))
    return sampled_field.astype(jnp.bfloat16)


def draw_rotated_key_rows(key, part):
    sampled_field = base_random_field(jax.random.fold_in(key, 2), (PROMPT_TOKENS, KEY_VALUE_HEADS * HEAD_SIZE))
    return sampled_field.astype(jnp.bfloat16)


def draw_live_blocks(key, part):
    first_key = jax.random.fold_in(key, 11)
    second_key = jax.random.fold_in(key, 12)
    row_ids = jnp.arange(PROMPT_BLOCKS, dtype=jnp.int32)
    uniform_pick = jax.random.randint(first_key, (PROMPT_BLOCKS,), 0, LIVE)
    wanted = LIVE - uniform_pick * uniform_pick // LIVE
    live_count = jnp.minimum(row_ids + 1, wanted)
    live_count = live_count.at[PROMPT_BLOCKS - 1].set(LIVE)
    col_ids = jnp.arange(PROMPT_BLOCKS, dtype=jnp.int32)
    ranked = jax.random.randint(second_key, (PROMPT_BLOCKS, PROMPT_BLOCKS), 0, 1 << 20) * PROMPT_BLOCKS + col_ids[None, :]
    ranked = jnp.where(col_ids[None, :] < row_ids[:, None], ranked, -1)
    top_values, earlier = jax.lax.top_k(ranked, LIVE - 1)
    slot_ids = jnp.arange(LIVE - 1, dtype=jnp.int32)
    entries = jnp.where(slot_ids[None, :] < live_count[:, None] - 1, earlier.astype(jnp.int32), -1)
    return jnp.concatenate([row_ids[:, None], entries], axis=1)


def block_levels(rng, dims, cuts, least, high):
    level = 1.0
    for dim, blocks in cuts:
        draws = jax.random.uniform(jax.random.fold_in(jax.random.fold_in(rng, 6), dim), (blocks,), jnp.float32, least / len(cuts), high / len(cuts))
        level = level * jnp.repeat(jnp.exp(draws), dims[dim] // blocks).reshape((-1,) + (1,) * (len(dims) - 1 - dim))
    return level


def scatter_about(stream_key, extent, deviation, reach, pieces=(), held_as=jnp.bfloat16):
    drawn = jax.random.normal(stream_key, extent, jnp.float32) * deviation
    if len(pieces) > 0:
        drawn = block_levels(stream_key, extent, pieces, -0.22, 0.18) * drawn
    return jnp.clip(drawn, min=-reach, max=reach).astype(held_as)


def setup_inputs(seed: int = 0, part: int = 0) -> dict:
    seeds = jax.random.split(jax.random.key(seed), 6)
    own_keys = jax.random.split(jax.random.fold_in(seeds[5], part), 6)
    return {
        "queries": draw_queries(jax.random.fold_in(jax.random.fold_in(seeds[5], part), 71), part),
        "rotated_key_rows": draw_rotated_key_rows(jax.random.fold_in(jax.random.fold_in(seeds[5], part), 71), part),
        "ordered_value_rows": scatter_about(own_keys[2], (PROMPT_TOKENS, KEY_VALUE_HEADS * HEAD_SIZE), 1.0, 6.0, ((0, 8), (1, 2))),
        "block_order": jax.random.permutation(own_keys[3], PROMPT_BLOCKS).astype(jnp.int32),
        "live_blocks": draw_live_blocks(jax.random.fold_in(jax.random.fold_in(seeds[5], part), 71), part),
    }


def reference(queries, rotated_key_rows, ordered_value_rows, block_order, live_blocks):
    query_groups = QUERY_HEADS // KEY_VALUE_HEADS
    factor = HEAD_SIZE ** -0.5
    block_ids = jnp.arange(PROMPT_BLOCKS, dtype=jnp.int32)
    inverse = jnp.zeros((PROMPT_BLOCKS,), jnp.int32).at[block_order].set(block_ids)
    blocked_keys = rotated_key_rows.reshape(PROMPT_BLOCKS, BLOCK_TOKENS, KEY_VALUE_HEADS, HEAD_SIZE)
    blocked_values = ordered_value_rows.reshape(PROMPT_BLOCKS, BLOCK_TOKENS, KEY_VALUE_HEADS, HEAD_SIZE)
    blocked_queries = queries.reshape(PROMPT_BLOCKS, BLOCK_TOKENS, KEY_VALUE_HEADS, query_groups, HEAD_SIZE)
    within = jnp.arange(BLOCK_TOKENS, dtype=jnp.int32)

    def one_block(index):
        seq_id = block_order[index]
        listed = live_blocks[seq_id]
        in_use = listed >= 0
        places = inverse[jnp.maximum(listed, 0)]
        picked_keys = blocked_keys[places].astype(jnp.float32)
        picked_values = blocked_values[places].astype(jnp.float32)
        query_part = blocked_queries[index].astype(jnp.float32)
        scores = jnp.einsum("qhgd,lkhd->hgqlk", query_part, picked_keys) * factor
        causal = within[None, None, :] <= within[:, None, None]
        allowed = in_use[None, :, None] & ((listed != seq_id)[None, :, None] | causal)
        scores = jnp.where(allowed, scores, -jnp.inf)
        row_peak = jnp.max(scores, axis=(3, 4))
        weights = jnp.where(allowed, jnp.exp(scores - row_peak[:, :, :, None, None]), 0.0)
        denominator = jnp.sum(weights, axis=(3, 4))
        rounded = lax.optimization_barrier(weights.astype(jnp.bfloat16)).astype(jnp.float32)
        summed = jnp.einsum("hgqlk,lkhd->hgqd", rounded, picked_values)
        normed = summed / denominator[..., None]
        merged_out = jnp.transpose(normed, (2, 0, 1, 3)).reshape(BLOCK_TOKENS, QUERY_HEADS * HEAD_SIZE).astype(jnp.bfloat16)
        norm_part = (row_peak + jnp.log(denominator)).reshape(QUERY_HEADS, BLOCK_TOKENS)
        return merged_out, norm_part

    out_blocks, norm_blocks = lax.map(one_block, block_ids)
    attended = out_blocks.reshape(PROMPT_TOKENS, QUERY_HEADS * HEAD_SIZE)
    log_norm = jnp.transpose(norm_blocks, (1, 0, 2)).reshape(QUERY_HEADS, PROMPT_TOKENS)
    return attended, log_norm
```

```python
import functools

import jax
import jax.numpy as jnp
import numpy as np
from jax import lax
from jax.experimental import pallas as pl
from jax.experimental.pallas import tpu as pltpu
from jax.sharding import PartitionSpec as P

HEAD_SIZE = 128
BLOCK_TOKENS = 128
SCALE2 = float(HEAD_SIZE**-0.5 * np.log2(np.e))
LN2 = float(np.log(2.0))
NEG_LARGE = -1e30
VMEM_BYTES = 24 * 2**20
CHUNK = 4


def attend(k, vt, qt_ref, qb, groups, mask, first, ml_ref, acc_ref):
    for g in range(groups):
        cols = slice(g * BLOCK_TOKENS, (g + 1) * BLOCK_TOKENS)
        scores = jnp.dot(k, qt_ref[qb, :, cols], preferred_element_type=jnp.float32) * SCALE2
        scores = mask(scores)
        peak = jnp.max(scores, axis=0, keepdims=True)
        if not first:
            old_peak = ml_ref[qb, 0, 0:1, cols]
            peak = jnp.maximum(peak, old_peak)
        weights = jnp.exp2(scores - peak)
        total = jnp.sum(weights, axis=0, keepdims=True)
        weighted = jnp.dot(vt, weights.astype(jnp.bfloat16), preferred_element_type=jnp.float32)
        if not first:
            rescale = jnp.exp2(old_peak - peak)
            total = total + ml_ref[qb, 0, 1:2, cols] * rescale
            weighted = weighted + acc_ref[qb, 0, :, cols] * rescale
        ml_ref[qb, 0, 0:1, cols] = peak
        ml_ref[qb, 0, 1:2, cols] = total
        acc_ref[qb, 0, :, cols] = weighted


def own_kernel(blocks, groups, table_ref, meta_ref, q_ref, k_ref, v_ref, qt_ref, ml_ref, acc_ref):
    me = meta_ref[0]
    rows = blocks * BLOCK_TOKENS
    vt = v_ref[...].T
    key_row = lax.broadcasted_iota(jnp.int32, (BLOCK_TOKENS, BLOCK_TOKENS), 0)
    query_col = lax.broadcasted_iota(jnp.int32, (BLOCK_TOKENS, BLOCK_TOKENS), 1)
    causal = key_row <= query_col
    for qb in range(blocks):
        for g in range(groups):
            cols = slice(g * BLOCK_TOKENS, (g + 1) * BLOCK_TOKENS)
            qt_ref[qb, :, cols] = q_ref[qb * BLOCK_TOKENS : (qb + 1) * BLOCK_TOKENS, cols].T

        def mask(scores):
            parts = []
            for j in range(blocks):
                part = scores[j * BLOCK_TOKENS : (j + 1) * BLOCK_TOKENS]
                keep = causal if j == qb else table_ref[qb, me * blocks + j] != 0
                parts.append(jnp.where(keep, part, NEG_LARGE))
            return jnp.concatenate(parts, axis=0)

        attend(k_ref[...], vt, qt_ref, qb, groups, mask, True, ml_ref, acc_ref)


def live_slots(masks, blocks, qb, table_ref, meta_ref, slot_ref):
    slots = len(masks) * blocks
    for t in range(slots + 1):
        slot_ref[t] = 0
    count = jnp.int32(0)
    for t in range(slots):
        owner = jnp.bitwise_xor(meta_ref[0], masks[t // blocks])
        slot_ref[count] = t
        count = count + table_ref[qb, owner * blocks + t % blocks]
    return count


def load_shards(shard_refs, blocks, k_buf, vt_buf):
    for i in range(len(shard_refs) // 2):
        for j in range(blocks):
            rows = slice(j * BLOCK_TOKENS, (j + 1) * BLOCK_TOKENS)
            k_buf[i * blocks + j] = shard_refs[2 * i][rows, :]
            vt_buf[i * blocks + j] = shard_refs[2 * i + 1][rows, :].T


def pairs_loop(count, slot_ref, k_buf, vt_buf, qt_ref, qb, groups, ml_ref, acc_ref):
    row = lax.broadcasted_iota(jnp.int32, (2 * BLOCK_TOKENS, BLOCK_TOKENS), 0)

    def step(p, carry):
        a, b = slot_ref[2 * p], slot_ref[2 * p + 1]
        used = jnp.minimum(count - 2 * p, 2) * BLOCK_TOKENS
        k = jnp.concatenate([k_buf[a], k_buf[b]], axis=0)
        vt = jnp.concatenate([vt_buf[a], vt_buf[b]], axis=1)
        mask = lambda scores: jnp.where(row < used, scores, NEG_LARGE)
        attend(k, vt, qt_ref, qb, groups, mask, False, ml_ref, acc_ref)
        return carry

    lax.fori_loop(0, (count + 1) // 2, step, 0)


def more_kernel(masks, blocks, groups, *refs):
    table_ref, meta_ref, qt_ref, ml_in, acc_in = refs[:5]
    shard_refs = refs[5 : 5 + 2 * len(masks)]
    ml_ref, acc_ref, slot_ref, k_buf, vt_buf = refs[5 + 2 * len(masks) :]
    load_shards(shard_refs, blocks, k_buf, vt_buf)
    for qb in range(blocks):
        ml_ref[qb] = ml_in[qb]
        acc_ref[qb] = acc_in[qb]
        count = live_slots(masks, blocks, qb, table_ref, meta_ref, slot_ref)
        pairs_loop(count, slot_ref, k_buf, vt_buf, qt_ref, qb, groups, ml_ref, acc_ref)


def last_kernel(masks, blocks, part, groups, *refs):
    table_ref, meta_ref, qt_ref, ml_in, acc_in = refs[:5]
    shard_refs = refs[5 : 5 + 2 * len(masks)]
    out_ref, norm_ref, ml_ref, acc_ref, slot_ref, k_buf, vt_buf = refs[5 + 2 * len(masks) :]
    load_shards(shard_refs, blocks, k_buf, vt_buf)
    for qb in range(part):
        ml_ref[qb] = ml_in[qb]
        acc_ref[qb] = acc_in[qb]
        count = live_slots(masks, blocks, meta_ref[1] * part + qb, table_ref, meta_ref, slot_ref)
        pairs_loop(count, slot_ref, k_buf, vt_buf, qt_ref, qb, groups, ml_ref, acc_ref)
        rows = slice(qb * BLOCK_TOKENS, (qb + 1) * BLOCK_TOKENS)
        for g in range(groups):
            cols = slice(g * BLOCK_TOKENS, (g + 1) * BLOCK_TOKENS)
            total = ml_ref[qb, 0, 1:2, cols]
            normed = acc_ref[qb, 0, :, cols] / total
            out_ref[rows, cols] = normed.astype(jnp.bfloat16).T
            norm_ref[g : g + 1, rows] = ml_ref[qb, 0, 0:1, cols] * LN2 + jnp.log(total)


def cost(tiles, groups, kv_local):
    flops = 4 * tiles * groups * kv_local * BLOCK_TOKENS * BLOCK_TOKENS * HEAD_SIZE
    return pl.CostEstimate(flops=4 * flops, bytes_accessed=4 * 2**20, transcendentals=0)


def body(queries, key_rows, value_rows, block_order, live_blocks):
    rows, width = queries.shape
    kv_local = key_rows.shape[1] // HEAD_SIZE
    groups = width // HEAD_SIZE // kv_local
    blocks = rows // BLOCK_TOKENS
    shards = lax.axis_size("ctx")
    cores = lax.axis_size("tp")
    part = blocks // cores
    wide = groups * HEAD_SIZE
    me = lax.axis_index("ctx")
    core = lax.axis_index("tp")

    shard = jnp.concatenate([key_rows, value_rows], axis=1)

    def swap(array, distance):
        return lax.ppermute(array, "ctx", [(i, i ^ distance) for i in range(shards)])

    my_blocks = lax.dynamic_slice_in_dim(block_order, me * blocks, blocks)
    lists = jnp.take(live_blocks, my_blocks, axis=0)
    table = jnp.any(lists[:, :, None] == block_order[None, None, :], axis=1).astype(jnp.int32)

    bits = [1 << i for i in range(shards.bit_length() - 1)]
    got = {0: shard}
    for bit in reversed(bits):
        got[bit] = swap(shard, bit)

    params = pltpu.CompilerParams(vmem_limit_bytes=VMEM_BYTES)
    qt_shape = jax.ShapeDtypeStruct((blocks, HEAD_SIZE, width), jnp.bfloat16)
    ml_shape = jax.ShapeDtypeStruct((blocks, kv_local, 2, wide), jnp.float32)
    acc_shape = jax.ShapeDtypeStruct((blocks, kv_local, HEAD_SIZE, wide), jnp.float32)
    meta = jnp.stack([me, core]).astype(jnp.int32)

    def kv_specs():
        return [
            pl.BlockSpec((rows, HEAD_SIZE), lambda i, *_: (0, i)),
            pl.BlockSpec((rows, HEAD_SIZE), lambda i, *_: (0, kv_local + i)),
        ]

    qt_spec = pl.BlockSpec((blocks, HEAD_SIZE, wide), lambda i, *_: (0, 0, i))
    ml_spec = pl.BlockSpec((blocks, 1, 2, wide), lambda i, *_: (0, i, 0, 0))
    acc_spec = pl.BlockSpec((blocks, 1, HEAD_SIZE, wide), lambda i, *_: (0, i, 0, 0))

    qt, ml, acc = pl.pallas_call(
        functools.partial(own_kernel, blocks, groups),
        grid_spec=pltpu.PrefetchScalarGridSpec(
            num_scalar_prefetch=2,
            grid=(kv_local,),
            in_specs=[pl.BlockSpec((rows, wide), lambda i, *_: (0, i))] + kv_specs(),
            out_specs=[qt_spec, ml_spec, acc_spec],
        ),
        out_shape=[qt_shape, ml_shape, acc_shape],
        compiler_params=params,
        cost_estimate=cost(blocks * blocks, groups, kv_local),
        name="own_shard",
    )(table, meta, queries, shard, shard)

    def buffers(masks):
        slots = len(masks) * blocks
        return [
            pltpu.SMEM((slots + 2,), jnp.int32),
            pltpu.VMEM((slots, BLOCK_TOKENS, HEAD_SIZE), jnp.bfloat16),
            pltpu.VMEM((slots, HEAD_SIZE, BLOCK_TOKENS), jnp.bfloat16),
        ]

    def more(masks, ml, acc):
        operands = [got[m] for m in masks for _ in range(2)]
        return pl.pallas_call(
            functools.partial(more_kernel, masks, blocks, groups),
            grid_spec=pltpu.PrefetchScalarGridSpec(
                num_scalar_prefetch=2,
                grid=(kv_local,),
                in_specs=[qt_spec, ml_spec, acc_spec] + kv_specs() * len(masks),
                out_specs=[ml_spec, acc_spec],
                scratch_shapes=buffers(masks),
            ),
            out_shape=[ml_shape, acc_shape],
            compiler_params=params,
            cost_estimate=cost(len(masks) * blocks * blocks, groups, kv_local),
            name="more_shards",
        )(table, meta, qt, ml, acc, *operands)

    def last(masks, which, ml, acc, whole):
        operands = [got[m] for m in masks for _ in range(2)]
        columns = cores * kv_local if whole else kv_local
        base = lambda meta_ref: meta_ref[1] * kv_local if whole else 0
        return pl.pallas_call(
            functools.partial(last_kernel, masks, blocks, part, groups),
            grid_spec=pltpu.PrefetchScalarGridSpec(
                num_scalar_prefetch=2,
                grid=(kv_local,),
                in_specs=[
                    pl.BlockSpec((part, HEAD_SIZE, wide), lambda i, t, w: (w[1], 0, i)),
                    pl.BlockSpec((part, 1, 2, wide), lambda i, t, w: (w[1], i, 0, 0)),
                    pl.BlockSpec((part, 1, HEAD_SIZE, wide), lambda i, t, w: (w[1], i, 0, 0)),
                ]
                + kv_specs() * len(masks),
                out_specs=[
                    pl.BlockSpec((part * BLOCK_TOKENS, wide), lambda i, t, w: (0, base(w) + i)),
                    pl.BlockSpec((groups, part * BLOCK_TOKENS), lambda i, t, w: (i, 0)),
                ],
                scratch_shapes=[
                    pltpu.VMEM((part, 1, 2, wide), jnp.float32),
                    pltpu.VMEM((part, 1, HEAD_SIZE, wide), jnp.float32),
                ]
                + buffers(masks),
            ),
            out_shape=[
                jax.ShapeDtypeStruct((part * BLOCK_TOKENS, columns * wide), jnp.bfloat16),
                jax.ShapeDtypeStruct((kv_local * groups, part * BLOCK_TOKENS), jnp.float32),
            ],
            compiler_params=params,
            cost_estimate=cost(len(masks) * blocks * part, groups, kv_local),
            name="last_shard",
        )(table, jnp.stack([me, which]).astype(jnp.int32), qt, ml, acc, *operands)

    pending = [1]
    for low in bits[1:]:
        relay = got[low] if low == 2 else lax.optimization_barrier((got[low], acc))[0]
        offsets = sorted(range(1, low), key=lambda o: (o.bit_count(), -o))
        for o in offsets:
            got[low + o] = swap(relay, o)
        if low > 2:
            pending = pending + [low]
        for i in range(0, len(pending), CHUNK):
            ml, acc = more(pending[i : i + CHUNK], ml, acc)
        pending = ([low] if low == 2 else []) + [low + o for o in offsets]
    for i in range(0, len(pending) - 1, CHUNK):
        ml, acc = more(pending[:-1][i : i + CHUNK], ml, acc)
    final = pending[-1:]

    sent, norms = {}, {}
    for step in range(cores - 1, 0, -1):
        to = lax.rem(core + step, cores)
        out, norms[step] = last(final, to, ml, acc, False)
        sent[step] = lax.ppermute(out, "tp", [(i, (i + step) % cores) for i in range(cores)])
    attended, norms[0] = last(final, core, ml, acc, True)
    log_norm = jnp.zeros((kv_local * groups, rows), jnp.float32)
    for step in range(cores):
        to = lax.rem(core + step, cores)
        log_norm = lax.dynamic_update_slice_in_dim(log_norm, norms[step], to * part * BLOCK_TOKENS, 1)
    for step in range(1, cores):
        origin = lax.rem(core - step + cores, cores)
        attended = lax.dynamic_update_slice_in_dim(attended, sent[step], origin * width, 1)
    return attended, log_norm


def solution(mesh):
    placed = (
        P(("rep", "ctx"), "tp"),
        P(("rep", "ctx"), "tp"),
        P(("rep", "ctx"), "tp"),
        P("rep"),
        P("rep", None),
    )
    return jax.shard_map(
        body,
        mesh=mesh,
        in_specs=placed,
        out_specs=(P(("rep", "ctx", "tp"), None), P(("rep", "tp"), "ctx")),
        check_vma=False,
    )
```

```python
import functools

import jax
import jax.numpy as jnp
import numpy as np
from jax import lax
from jax.experimental import pallas as pl
from jax.experimental.pallas import tpu as pltpu
from jax.sharding import PartitionSpec as P

HEAD_SIZE = 128
BLOCK_TOKENS = 128
SCALE2 = float(HEAD_SIZE**-0.5 * np.log2(np.e))
LN2 = float(np.log(2.0))
FAR = 1e30
VMEM_BYTES = 24 * 2**20
FULL_VMEM = 64 * 2**20
COST = 1024
CHUNK = 2


def tile(i):
    return slice(i * BLOCK_TOKENS, (i + 1) * BLOCK_TOKENS)


def attend(shard_ref, qb, place, gaps, diagonal, kv_local, groups, qt_ref, ml_ref, acc_ref):
    blocks = len(gaps)
    first = diagonal is not None
    keys = [shard_ref[0 : blocks * BLOCK_TOKENS, tile(i)] for i in range(kv_local)]
    values = [
        jnp.concatenate([shard_ref[tile(blocks + j), tile(i)] for j in range(blocks)], axis=1)
        for i in range(kv_local)
    ]
    if first:
        key_row = lax.broadcasted_iota(jnp.int32, (BLOCK_TOKENS, BLOCK_TOKENS), 0)
        query_col = lax.broadcasted_iota(jnp.int32, (BLOCK_TOKENS, BLOCK_TOKENS), 1)
        causal = key_row <= query_col
    heads = [i * groups + g for g in range(groups) for i in range(kv_local)]
    scores, weights, rescales = {}, {}, {}

    def score(h):
        scores[h] = jnp.dot(keys[h // groups], qt_ref[qb, :, tile(h)], preferred_element_type=jnp.float32)

    def soften(h):
        whole = scores.pop(h)
        parts = [whole[tile(j)] * SCALE2 for j in range(blocks)]
        if first:
            parts[diagonal] = jnp.where(causal, parts[diagonal], -FAR)
        peak = functools.reduce(
            jnp.maximum, [jnp.max(part, axis=0, keepdims=True) - gap for part, gap in zip(parts, gaps)]
        )
        if not first:
            old_peak = ml_ref[place, 0:1, tile(h)]
            peak = jnp.maximum(peak, old_peak)
        exps = [jnp.exp2(part - (peak + gap)) for part, gap in zip(parts, gaps)]
        total = functools.reduce(jnp.add, [jnp.sum(e, axis=0, keepdims=True) for e in exps])
        if not first:
            rescales[h] = jnp.exp2(old_peak - peak)
            total = total + ml_ref[place, 1:2, tile(h)] * rescales[h]
        ml_ref[place, 0:1, tile(h)] = peak
        ml_ref[place, 1:2, tile(h)] = total
        weights[h] = jnp.concatenate([e.astype(jnp.bfloat16) for e in exps], axis=0)

    def weigh(h):
        weighted = jnp.dot(values[h // groups], weights.pop(h), preferred_element_type=jnp.float32)
        if not first:
            weighted = weighted + acc_ref[place, :, tile(h)] * rescales.pop(h)
        acc_ref[place, :, tile(h)] = weighted

    for t in range(len(heads) + 2):
        if t < len(heads):
            score(heads[t])
        if 1 <= t <= len(heads):
            soften(heads[t - 1])
        if t >= 2:
            weigh(heads[t - 2])


def attend_shards(masks, blocks, query_blocks, flags_ref, shard_refs, **rest):
    me = lax.axis_index("ctx")
    total = flags_ref.shape[0] // blocks
    for m, shard_ref in zip(masks, shard_refs):
        for qb, place in query_blocks:
            mine = [flags_ref[qb * total + (me ^ m) * blocks + j] for j in range(blocks)]

            @pl.when(functools.reduce(jnp.bitwise_or, mine) != 0)
            def _():
                gaps = [jnp.where(flag != 0, 0.0, FAR) for flag in mine]
                attend(shard_ref, qb, place, gaps, None, **rest)


def pack_kernel(blocks, k_hbm, v_hbm, order_hbm, live_hbm, shard_ref, flags_ref, v_buf, order_ref, live_ref, place_ref, sems):
    rows, width = v_buf.shape
    total, slots = order_ref.shape[0], live_ref.shape[1]
    pairs = [(v_hbm, v_buf), (k_hbm, shard_ref.at[0:rows, :]), (order_hbm, order_ref), (live_hbm, live_ref)]
    copies = [pltpu.make_async_copy(source, target, sems.at[i]) for i, (source, target) in enumerate(pairs)]
    for copy in copies:
        copy.start()

    def clear(i, carry):
        flags_ref[i] = 0
        return carry

    def invert(b, carry):
        place_ref[order_ref[b]] = b
        return carry

    lax.fori_loop(0, blocks * total, clear, 0, unroll=8)
    copies[2].wait()
    lax.fori_loop(0, total, invert, 0, unroll=8)
    copies[3].wait()
    me = lax.axis_index("ctx")
    for qb in range(blocks):
        row = order_ref[me * blocks + qb]

        def mark(slot, carry):
            entry = live_ref[row, slot]
            spot = qb * total + place_ref[jnp.maximum(entry, 0)]
            flags_ref[jnp.where(entry >= 0, spot, blocks * total)] = 1
            return carry

        lax.fori_loop(0, slots, mark, 0, unroll=4)
    copies[0].wait()
    for j in range(rows // BLOCK_TOKENS):
        for i in range(width // HEAD_SIZE):
            shard_ref[tile(rows // BLOCK_TOKENS + j), tile(i)] = v_buf[tile(j), tile(i)].T
    copies[1].wait()


def tick_kernel(_shard, tick_ref):
    tick_ref[0] = 0


def own_kernel(masks, blocks, kv_local, groups, flags_ref, q_ref, own_ref, *refs):
    shard_refs, (qt_ref, ml_ref, acc_ref) = refs[: len(masks)], refs[len(masks) :]
    me = lax.axis_index("ctx")
    total = flags_ref.shape[0] // blocks
    for qb in range(blocks):
        for h in range(kv_local * groups):
            qt_ref[qb, :, tile(h)] = q_ref[tile(qb), tile(h)].T
        flags = [flags_ref[qb * total + me * blocks + j] for j in range(blocks)]
        gaps = [0.0 if j == qb else jnp.where(flags[j] != 0, 0.0, FAR) for j in range(blocks)]
        attend(own_ref, qb, qb, gaps, qb, kv_local, groups, qt_ref, ml_ref, acc_ref)
    attend_shards(
        masks, blocks, [(qb, qb) for qb in range(blocks)], flags_ref, shard_refs,
        kv_local=kv_local, groups=groups, qt_ref=qt_ref, ml_ref=ml_ref, acc_ref=acc_ref,
    )


def more_kernel(masks, blocks, kv_local, groups, flags_ref, qt_ref, ml_in, acc_in, *refs):
    shard_refs, (ml_ref, acc_ref) = refs[: len(masks)], refs[len(masks) :]
    ml_ref[...] = ml_in[...]
    acc_ref[...] = acc_in[...]
    attend_shards(
        masks, blocks, [(qb, qb) for qb in range(blocks)], flags_ref, shard_refs,
        kv_local=kv_local, groups=groups, qt_ref=qt_ref, ml_ref=ml_ref, acc_ref=acc_ref,
    )


def last_kernel(masks, blocks, part, step, cores, kv_local, groups, flags_ref, qt_ref, ml_in, acc_in, *refs):
    shard_refs, refs = refs[: len(masks)], refs[len(masks) :]
    core = lax.axis_index("tp")
    if step:
        out_ref, norm_ref, ml_ref, acc_ref = refs
    else:
        others, (out_hbm, norm_hbm, out_ref, norm_ref, ml_ref, acc_ref, sems) = refs[: cores - 1], refs[cores - 1 :]
    heads = kv_local * groups

    def columns(to, j):
        first = (to * part + j) * BLOCK_TOKENS
        return pl.ds(pl.multiple_of(first, BLOCK_TOKENS), BLOCK_TOKENS)

    if not step:
        for i, other in enumerate(others):
            for j in range(part):
                norm_ref[:, columns(lax.rem(core + i + 1, cores), j)] = other[:, tile(j)]
    to = lax.rem(core + step, cores)
    query_blocks = [(to * part + j, j) for j in range(part)]
    for qb, j in query_blocks:
        ml_ref[j] = ml_in[qb]
        acc_ref[j] = acc_in[qb]
    attend_shards(
        masks, blocks, query_blocks, flags_ref, shard_refs,
        kv_local=kv_local, groups=groups, qt_ref=qt_ref, ml_ref=ml_ref, acc_ref=acc_ref,
    )
    copies = []
    width = out_ref.shape[1]
    for h in range(heads):
        for j in range(part):
            total = ml_ref[j, 1:2, tile(h)]
            normed = acc_ref[j, :, tile(h)] * (1.0 / total)
            out_ref[tile(j), tile(h)] = normed.astype(jnp.bfloat16).T
            norm = ml_ref[j, 0:1, tile(h)] * LN2 + jnp.log(total)
            if step:
                norm_ref[h : h + 1, tile(j)] = norm
            else:
                norm_ref[h : h + 1, columns(to, j)] = norm
        if not step and (h + 1) % groups == 0:
            i = h // groups
            mine = slice(i * groups * HEAD_SIZE, (i + 1) * groups * HEAD_SIZE)
            start = pl.multiple_of(to * width + mine.start, HEAD_SIZE)
            copies.append(
                pltpu.make_async_copy(
                    out_ref.at[:, mine], out_hbm.at[:, pl.ds(start, groups * HEAD_SIZE)], sems.at[i]
                )
            )
            copies[-1].start()
    if not step:
        copies.append(pltpu.make_async_copy(norm_ref, norm_hbm, sems.at[kv_local]))
        copies[-1].start()
    for copy in copies:
        copy.wait()


def place_kernel(step, cores, _out, sent_ref, out_hbm, sem):
    width = sent_ref.shape[1]
    origin = lax.rem(lax.axis_index("tp") + cores - step, cores)
    start = pl.multiple_of(origin * width, width)
    copy = pltpu.make_async_copy(sent_ref, out_hbm.at[:, pl.ds(start, width)], sem)
    copy.start()
    copy.wait()


def body(queries, key_rows, value_rows, block_order, live_blocks):
    rows, width = queries.shape
    kv_local = key_rows.shape[1] // HEAD_SIZE
    heads = width // HEAD_SIZE
    groups = heads // kv_local
    blocks = rows // BLOCK_TOKENS
    shards = lax.axis_size("ctx")
    cores = lax.axis_size("tp")
    part = blocks // cores

    vmem = pl.BlockSpec(memory_space=pltpu.VMEM)
    smem = pl.BlockSpec(memory_space=pltpu.SMEM)
    hbm = pl.BlockSpec(memory_space=pltpu.HBM)
    qt_shape = jax.ShapeDtypeStruct((blocks, HEAD_SIZE, width), jnp.bfloat16)
    ml_shape = jax.ShapeDtypeStruct((blocks, 2, width), jnp.float32)
    acc_shape = jax.ShapeDtypeStruct((blocks, HEAD_SIZE, width), jnp.float32)

    def call(kernel, name, limit=VMEM_BYTES, **options):
        return pl.pallas_call(
            kernel,
            name=name,
            compiler_params=pltpu.CompilerParams(vmem_limit_bytes=limit),
            cost_estimate=pl.CostEstimate(flops=COST, bytes_accessed=COST, transcendentals=0),
            **options,
        )

    def swap(array, distance):
        return lax.ppermute(array, "ctx", [(i, i ^ distance) for i in range(shards)])

    shard, flags = call(
        functools.partial(pack_kernel, blocks),
        "pack",
        FULL_VMEM,
        in_specs=[hbm] * 4,
        out_specs=[vmem, smem],
        out_shape=[
            jax.ShapeDtypeStruct((2 * rows, kv_local * HEAD_SIZE), jnp.bfloat16),
            jax.ShapeDtypeStruct((blocks * block_order.shape[0] + 1,), jnp.int32),
        ],
        scratch_shapes=[
            pltpu.VMEM(value_rows.shape, jnp.bfloat16),
            pltpu.SMEM(block_order.shape, jnp.int32),
            pltpu.SMEM(live_blocks.shape, jnp.int32),
            pltpu.SMEM(block_order.shape, jnp.int32),
            pltpu.SemaphoreType.DMA((4,)),
        ],
    )(key_rows, value_rows, block_order, live_blocks)
    bits = [1 << i for i in range(shards.bit_length() - 1)]
    got = {bits[-1]: swap(shard, bits[-1])}
    tick = call(
        tick_kernel,
        "tick",
        FULL_VMEM,
        in_specs=[hbm],
        out_specs=smem,
        out_shape=jax.ShapeDtypeStruct((1,), jnp.int32),
    )(shard)
    later = lax.optimization_barrier((shard, tick))[0]
    for bit in bits[:-1]:
        got[bit] = swap(later, bit)

    qt, ml, acc = call(
        functools.partial(own_kernel, [], blocks, kv_local, groups),
        "own_shard",
        in_specs=[smem] + [vmem] * 2,
        out_specs=[vmem] * 3,
        out_shape=[qt_shape, ml_shape, acc_shape],
    )(flags, queries, shard)

    def more(masks, ml, acc):
        return call(
            functools.partial(more_kernel, masks, blocks, kv_local, groups),
            "more_shards",
            in_specs=[smem] + [vmem] * (3 + len(masks)),
            out_specs=[vmem] * 2,
            out_shape=[ml_shape, acc_shape],
        )(flags, qt, ml, acc, *[got[m] for m in masks])

    def last(masks, step, ml, acc, norms):
        rows_out = part * BLOCK_TOKENS
        out_shape = jax.ShapeDtypeStruct((rows_out, width if step else cores * width), jnp.bfloat16)
        norm_shape = jax.ShapeDtypeStruct((heads, rows_out if step else rows), jnp.float32)
        scratch = [
            pltpu.VMEM((part, *ml_shape.shape[1:]), jnp.float32),
            pltpu.VMEM((part, *acc_shape.shape[1:]), jnp.float32),
        ]
        if not step:
            scratch = [pltpu.VMEM((rows_out, width), jnp.bfloat16), pltpu.VMEM((heads, rows), jnp.float32)] + scratch
            scratch.append(pltpu.SemaphoreType.DMA((kv_local + 1,)))
        return call(
            functools.partial(last_kernel, masks, blocks, part, step, cores, kv_local, groups),
            "last_shards",
            in_specs=[smem] + [vmem] * (3 + len(masks) + len(norms)),
            out_specs=[vmem, vmem] if step else [hbm, hbm],
            out_shape=[out_shape, norm_shape],
            scratch_shapes=scratch,
        )(flags, qt, ml, acc, *[got[m] for m in masks], *norms)

    several = sorted((m for m in range(shards) if m.bit_count() > 1), key=lambda m: (m.bit_count(), m))
    if 3 in several[:-1]:
        several.remove(3)
        several.insert(len(several) - 1, 3)
    ml, acc = more(bits[:1], ml, acc)
    relays = {bit: lax.optimization_barrier((got[bit], acc))[0] for bit in bits}
    for m in several:
        if m != 3:
            low = m & -m
            got[m] = swap(relays.get(m - low, got.get(m - low)), low)
    for i in range(1, len(bits), CHUNK):
        ml, acc = more(bits[i : i + CHUNK], ml, acc)
    if 3 in several:
        got[3] = swap(lax.optimization_barrier((got[1], acc))[0], 2)
    tail = max(len(several) - 2, 0)
    for i in range(0, tail, CHUNK):
        ml, acc = more(several[:tail][i : i + CHUNK], ml, acc)
    final = several[tail:]

    sent, norms = {}, {}
    for step in range(cores - 1, 0, -1):
        out, norms[step] = last(final, step, ml, acc, [])
        sent[step] = lax.ppermute(out, "tp", [(i, (i + step) % cores) for i in range(cores)])
    out, norm = last(final, 0, ml, acc, [norms[step] for step in range(1, cores)])
    for step in range(1, cores):
        out = call(
            functools.partial(place_kernel, step, cores),
            "place",
            in_specs=[hbm, vmem],
            out_specs=hbm,
            out_shape=jax.ShapeDtypeStruct(out.shape, out.dtype),
            input_output_aliases={0: 0},
            scratch_shapes=[pltpu.SemaphoreType.DMA],
        )(out, sent[step])
    return out, norm


def solution(mesh):
    placed = (
        P(("rep", "ctx"), "tp"),
        P(("rep", "ctx"), "tp"),
        P(("rep", "ctx"), "tp"),
        P("rep"),
        P("rep", None),
    )
    return jax.shard_map(
        body,
        mesh=mesh,
        in_specs=placed,
        out_specs=(P(("rep", "ctx", "tp"), None), P(("rep", "tp"), "ctx")),
        check_vma=False,
    )
```

```python
import functools

import jax
import jax.numpy as jnp
import numpy as np
from jax import lax
from jax.experimental import pallas as pl
from jax.experimental.pallas import tpu as pltpu
from jax.sharding import PartitionSpec as P

HEAD_SIZE = 128
BLOCK_TOKENS = 128
SCALE2 = float(HEAD_SIZE**-0.5 * np.log2(np.e))
LN2 = float(np.log(2.0))
FAR = 1e30
VMEM_BYTES = 24 * 2**20
FULL_VMEM = 64 * 2**20
COST = 1024
CHUNK = 3


def tile(i):
    return slice(i * BLOCK_TOKENS, (i + 1) * BLOCK_TOKENS)


def attend(shard, qb, place, gaps, diagonal, kv_local, groups, qt_ref, ml_ref, acc_ref, finish=None):
    blocks = len(gaps)
    first = diagonal is not None
    keys_ref, values_ref = shard
    keys = [keys_ref[:, tile(i)] for i in range(kv_local)]
    values = [
        jnp.concatenate([values_ref[tile(j), tile(i)] for j in range(blocks)], axis=1) for i in range(kv_local)
    ]
    if first:
        key_row = lax.broadcasted_iota(jnp.int32, (BLOCK_TOKENS, BLOCK_TOKENS), 0)
        query_col = lax.broadcasted_iota(jnp.int32, (BLOCK_TOKENS, BLOCK_TOKENS), 1)
        causal = key_row <= query_col
    heads = [i * groups + g for g in range(groups) for i in range(kv_local)]
    scores, weights, rescales, ends = {}, {}, {}, {}

    def score(h):
        scores[h] = jnp.dot(keys[h // groups], qt_ref[qb, :, tile(h)], preferred_element_type=jnp.float32)

    def soften(h):
        whole = scores.pop(h)
        parts = [whole[tile(j)] * SCALE2 for j in range(blocks)]
        if first:
            parts[diagonal] = jnp.where(causal, parts[diagonal], -FAR)
        peak = functools.reduce(
            jnp.maximum, [jnp.max(part, axis=0, keepdims=True) - gap for part, gap in zip(parts, gaps)]
        )
        if not first:
            old_peak = ml_ref[place, 0:1, tile(h)]
            peak = jnp.maximum(peak, old_peak)
        exps = [jnp.exp2(part - (peak + gap)) for part, gap in zip(parts, gaps)]
        total = functools.reduce(jnp.add, [jnp.sum(e, axis=0, keepdims=True) for e in exps])
        if not first:
            rescales[h] = jnp.exp2(old_peak - peak)
            total = total + ml_ref[place, 1:2, tile(h)] * rescales[h]
        if finish:
            ends[h] = peak, total
        else:
            ml_ref[place, 0:1, tile(h)] = peak
            ml_ref[place, 1:2, tile(h)] = total
        weights[h] = jnp.concatenate([e.astype(jnp.bfloat16) for e in exps], axis=0)

    def weigh(h):
        weighted = jnp.dot(values[h // groups], weights.pop(h), preferred_element_type=jnp.float32)
        if not first:
            weighted = weighted + acc_ref[place, :, tile(h)] * rescales.pop(h)
        if finish:
            finish(h, *ends.pop(h), weighted)
        else:
            acc_ref[place, :, tile(h)] = weighted

    for t in range(len(heads) + 2):
        if t < len(heads):
            score(heads[t])
        if 1 <= t <= len(heads):
            soften(heads[t - 1])
        if t >= 2:
            weigh(heads[t - 2])


def split_shards(pieces, refs):
    shards, refs = [], list(refs)
    for count in pieces:
        if count == 2:
            shards.append((refs.pop(0), refs.pop(0)))
        else:
            shards.append(halves(refs.pop(0)))
    return shards, refs


def halves(shard_ref):
    rows = shard_ref.shape[0] // 2
    return shard_ref.at[0:rows, :], shard_ref.at[rows : 2 * rows, :]


def attend_shards(masks, blocks, first, count, flags_ref, shards, **rest):
    me = lax.axis_index("ctx")
    total = flags_ref.shape[0] // blocks
    for m, shard in zip(masks, shards):

        def step(place, carry):
            qb = first + place
            mine = [flags_ref[qb * total + (me ^ m) * blocks + j] for j in range(blocks)]

            @pl.when(functools.reduce(jnp.bitwise_or, mine) != 0)
            def _():
                gaps = [jnp.where(flag != 0, 0.0, FAR) for flag in mine]
                attend(shard, qb, place, gaps, None, **rest)

            return carry

        if count == 1:
            step(0, 0)
        else:
            lax.fori_loop(0, count, step, 0)


def pack_kernel(blocks, k_hbm, v_hbm, order_hbm, live_hbm, shard_ref, values_ref, flags_ref, v_buf, order_ref, live_ref, place_ref, sems):
    rows, width = v_buf.shape
    total, slots = order_ref.shape[0], live_ref.shape[1]
    pairs = [(v_hbm, v_buf), (k_hbm, shard_ref.at[0:rows, :]), (order_hbm, order_ref), (live_hbm, live_ref)]
    copies = [pltpu.make_async_copy(source, target, sems.at[i]) for i, (source, target) in enumerate(pairs)]
    for copy in copies:
        copy.start()

    def clear(i, carry):
        flags_ref[i] = 0
        return carry

    def invert(b, carry):
        place_ref[order_ref[b]] = b
        return carry

    lax.fori_loop(0, blocks * total, clear, 0, unroll=8)
    copies[2].wait()
    lax.fori_loop(0, total, invert, 0, unroll=8)
    copies[3].wait()
    me = lax.axis_index("ctx")
    for qb in range(blocks):
        row = order_ref[me * blocks + qb]

        def mark(slot, carry):
            entry = live_ref[row, slot]
            spot = qb * total + place_ref[jnp.maximum(entry, 0)]
            flags_ref[jnp.where(entry >= 0, spot, blocks * total)] = 1
            return carry

        lax.fori_loop(0, slots, mark, 0, unroll=4)
    copies[0].wait()
    for j in range(rows // BLOCK_TOKENS):
        for i in range(width // HEAD_SIZE):
            turned = v_buf[tile(j), tile(i)].T
            shard_ref[tile(rows // BLOCK_TOKENS + j), tile(i)] = turned
            values_ref[tile(j), tile(i)] = turned
    copies[1].wait()


def tick_kernel(_shard, tick_ref):
    tick_ref[0] = 0


def own_kernel(blocks, kv_local, groups, flags_ref, q_ref, own_ref, qt_ref, ml_ref, acc_ref):
    me = lax.axis_index("ctx")
    total = flags_ref.shape[0] // blocks
    for qb in range(blocks):
        for h in range(kv_local * groups):
            qt_ref[qb, :, tile(h)] = q_ref[tile(qb), tile(h)].T
        flags = [flags_ref[qb * total + me * blocks + j] for j in range(blocks)]
        gaps = [0.0 if j == qb else jnp.where(flags[j] != 0, 0.0, FAR) for j in range(blocks)]
        attend(halves(own_ref), qb, qb, gaps, qb, kv_local, groups, qt_ref, ml_ref, acc_ref)


def more_kernel(masks, pieces, blocks, kv_local, groups, flags_ref, qt_ref, ml_in, acc_in, *refs):
    shards, (ml_ref, acc_ref) = split_shards(pieces, refs)
    ml_ref[...] = ml_in[...]
    acc_ref[...] = acc_in[...]
    attend_shards(
        masks, blocks, 0, blocks, flags_ref, shards,
        kv_local=kv_local, groups=groups, qt_ref=qt_ref, ml_ref=ml_ref, acc_ref=acc_ref,
    )


def last_kernel(masks, pieces, blocks, part, step, cores, kv_local, groups, flags_ref, qt_ref, ml_in, acc_in, *refs):
    shards, (out_ref, norm_ref, ml_ref, acc_ref) = split_shards(pieces, refs)
    to = lax.rem(lax.axis_index("tp") + step, cores)
    for j in range(part):
        ml_ref[j] = ml_in[to * part + j]
        acc_ref[j] = acc_in[to * part + j]
    rest = dict(kv_local=kv_local, groups=groups, qt_ref=qt_ref, ml_ref=ml_ref, acc_ref=acc_ref)
    attend_shards(masks[:-1], blocks, to * part, part, flags_ref, shards[:-1], **rest)
    me = lax.axis_index("ctx")
    total = flags_ref.shape[0] // blocks
    for j in range(part):

        def finish(h, peak, denominator, weighted):
            normed = weighted * (1.0 / denominator)
            out_ref[tile(j), tile(h)] = normed.astype(jnp.bfloat16).T
            norm_ref[h : h + 1, tile(j)] = peak * LN2 + jnp.log(denominator)

        qb = to * part + j
        mine = [flags_ref[qb * total + (me ^ masks[-1]) * blocks + b] for b in range(blocks)]
        some = functools.reduce(jnp.bitwise_or, mine)

        @pl.when(some != 0)
        def _():
            gaps = [jnp.where(flag != 0, 0.0, FAR) for flag in mine]
            attend(shards[-1], qb, j, gaps, None, finish=finish, **rest)

        @pl.when(some == 0)
        def _():
            for h in range(kv_local * groups):
                finish(h, ml_ref[j, 0:1, tile(h)], ml_ref[j, 1:2, tile(h)], acc_ref[j, :, tile(h)])


def place_kernel(cores, *refs):
    outs, norms, (out_hbm, norm_hbm, sems) = refs[:cores], refs[cores : 2 * cores], refs[2 * cores :]
    core = lax.axis_index("tp")
    copies = []
    for step in range(cores):
        origin = lax.rem(core + cores - step, cores)
        width = outs[step].shape[1]
        columns = pl.ds(pl.multiple_of(origin * width, HEAD_SIZE), width)
        copies.append(pltpu.make_async_copy(outs[step], out_hbm.at[:, columns], sems.at[step]))
    for step in range(cores):
        to = lax.rem(core + step, cores)
        width = norms[step].shape[1]
        columns = pl.ds(pl.multiple_of(to * width, BLOCK_TOKENS), width)
        copies.append(pltpu.make_async_copy(norms[step], norm_hbm.at[:, columns], sems.at[cores + step]))
    for copy in copies:
        copy.start()
    for copy in copies:
        copy.wait()


def body(queries, key_rows, value_rows, block_order, live_blocks):
    rows, width = queries.shape
    kv_local = key_rows.shape[1] // HEAD_SIZE
    heads = width // HEAD_SIZE
    groups = heads // kv_local
    blocks = rows // BLOCK_TOKENS
    shards = lax.axis_size("ctx")
    cores = lax.axis_size("tp")
    part = blocks // cores

    vmem = pl.BlockSpec(memory_space=pltpu.VMEM)
    smem = pl.BlockSpec(memory_space=pltpu.SMEM)
    hbm = pl.BlockSpec(memory_space=pltpu.HBM)
    qt_shape = jax.ShapeDtypeStruct((blocks, HEAD_SIZE, width), jnp.bfloat16)
    ml_shape = jax.ShapeDtypeStruct((blocks, 2, width), jnp.float32)
    acc_shape = jax.ShapeDtypeStruct((blocks, HEAD_SIZE, width), jnp.float32)

    def call(kernel, name, limit=VMEM_BYTES, **options):
        return pl.pallas_call(
            kernel,
            name=name,
            compiler_params=pltpu.CompilerParams(vmem_limit_bytes=limit),
            cost_estimate=pl.CostEstimate(flops=COST, bytes_accessed=COST, transcendentals=0),
            **options,
        )

    def swap(array, distance):
        return lax.ppermute(array, "ctx", [(i, i ^ distance) for i in range(shards)])

    bits = [1 << i for i in range(shards.bit_length() - 1)]
    top = bits[-1]
    shard, values, flags = call(
        functools.partial(pack_kernel, blocks),
        "pack",
        FULL_VMEM,
        in_specs=[hbm] * 4,
        out_specs=[vmem, vmem, smem],
        out_shape=[
            jax.ShapeDtypeStruct((2 * rows, kv_local * HEAD_SIZE), jnp.bfloat16),
            jax.ShapeDtypeStruct((rows, kv_local * HEAD_SIZE), jnp.bfloat16),
            jax.ShapeDtypeStruct((blocks * block_order.shape[0] + 1,), jnp.int32),
        ],
        scratch_shapes=[
            pltpu.VMEM(value_rows.shape, jnp.bfloat16),
            pltpu.SMEM(block_order.shape, jnp.int32),
            pltpu.SMEM(live_blocks.shape, jnp.int32),
            pltpu.SMEM(block_order.shape, jnp.int32),
            pltpu.SemaphoreType.DMA((4,)),
        ],
    )(key_rows, value_rows, block_order, live_blocks)
    got = {top: [swap(shard, top)]}
    for bit in reversed(bits[1:-1]):
        got[bit] = [swap(shard, bit)]
    got[1] = [swap(key_rows, 1), swap(values, 1)]

    qt, ml, acc = call(
        functools.partial(own_kernel, blocks, kv_local, groups),
        "own_shard",
        in_specs=[smem] + [vmem] * 2,
        out_specs=[vmem] * 3,
        out_shape=[qt_shape, ml_shape, acc_shape],
    )(flags, queries, shard)

    def more(masks, ml, acc):
        return call(
            functools.partial(more_kernel, masks, [len(got[m]) for m in masks], blocks, kv_local, groups),
            "more_shards",
            in_specs=[smem] + [vmem] * (3 + sum(len(got[m]) for m in masks)),
            out_specs=[vmem] * 2,
            out_shape=[ml_shape, acc_shape],
        )(flags, qt, ml, acc, *[array for m in masks for array in got[m]])

    def last(masks, step, ml, acc):
        arrays = [array for m in masks for array in got[m]]
        return call(
            functools.partial(
                last_kernel, masks, [len(got[m]) for m in masks], blocks, part, step, cores, kv_local, groups
            ),
            "last_shards",
            in_specs=[smem] + [vmem] * (3 + len(arrays)),
            out_specs=[vmem, vmem],
            out_shape=[
                jax.ShapeDtypeStruct((part * BLOCK_TOKENS, width), jnp.bfloat16),
                jax.ShapeDtypeStruct((heads, part * BLOCK_TOKENS), jnp.float32),
            ],
            scratch_shapes=[
                pltpu.VMEM((part, *ml_shape.shape[1:]), jnp.float32),
                pltpu.VMEM((part, *acc_shape.shape[1:]), jnp.float32),
            ],
        )(flags, qt, ml, acc, *arrays)

    def after(arrays, *others):
        return [lax.optimization_barrier((array,) + others)[0] for array in arrays]

    several = sorted((m for m in range(shards) if m.bit_count() > 1), key=lambda m: (m.bit_count(), m))
    ml, acc = more([1], ml, acc)
    got[top] = after(got[top], acc)
    for bit in reversed(bits[1:-1]):
        got[bit] = after(got[bit], got[top][0])
        got[top] = after(got[top], got[bit][0])
    for m in several:
        if m & top and m.bit_count() == 2:
            got[m] = [swap(array, m & -m) for array in got[m & (m - 1)]]
    ml, acc = more(bits[1:], ml, acc)
    got[3] = [swap(jnp.concatenate(after(got[1], acc), axis=0), 2)]
    for m in several:
        if m not in got:
            got[m] = [swap(array, m & -m) for array in after(got[m & (m - 1)], acc)]
    final = [3, several[-1]]
    ready = [m for m in several if m not in final]
    for i in range(0, len(ready), CHUNK):
        ml, acc = more(ready[i : i + CHUNK], ml, acc)

    outs, norms = [None] * cores, [None] * cores
    for step in range(cores - 1, -1, -1):
        outs[step], norms[step] = last(final, step, ml, acc)
        if step:
            outs[step] = lax.ppermute(outs[step], "tp", [(i, (i + step) % cores) for i in range(cores)])
    return call(
        functools.partial(place_kernel, cores),
        "place",
        in_specs=[vmem] * (2 * cores),
        out_specs=[hbm, hbm],
        out_shape=[
            jax.ShapeDtypeStruct((part * BLOCK_TOKENS, cores * width), jnp.bfloat16),
            jax.ShapeDtypeStruct((heads, rows), jnp.float32),
        ],
        scratch_shapes=[pltpu.SemaphoreType.DMA((2 * cores,))],
    )(*outs, *norms)


def solution(mesh):
    placed = (
        P(("rep", "ctx"), "tp"),
        P(("rep", "ctx"), "tp"),
        P(("rep", "ctx"), "tp"),
        P("rep"),
        P("rep", None),
    )
    return jax.shard_map(
        body,
        mesh=mesh,
        in_specs=placed,
        out_specs=(P(("rep", "ctx", "tp"), None), P(("rep", "tp"), "ctx")),
        check_vma=False,
    )
```

```python
import functools

import jax
import jax.numpy as jnp
import numpy as np
from jax import lax
from jax.experimental import pallas as pl
from jax.experimental.pallas import tpu as pltpu
from jax.sharding import PartitionSpec as P

HEAD_SIZE = 128
BLOCK_TOKENS = 128
SCALE2 = float(HEAD_SIZE**-0.5 * np.log2(np.e))
LN2 = float(np.log(2.0))
FAR = 1e30
VMEM_BYTES = 24 * 2**20
COST = 1024
CHUNK = 3


def tile(i):
    return slice(i * BLOCK_TOKENS, (i + 1) * BLOCK_TOKENS)


def attend(shard, qb, place, gaps, diagonal, kv_local, groups, qt_ref, ml_ref, acc_ref, finish=None):
    blocks = len(gaps)
    first = diagonal is not None
    keys_ref, values_ref = shard
    keys = [keys_ref[:, tile(i)] for i in range(kv_local)]
    values = [
        jnp.concatenate([values_ref[tile(j), tile(i)] for j in range(blocks)], axis=1) for i in range(kv_local)
    ]
    if first:
        key_row = lax.broadcasted_iota(jnp.int32, (BLOCK_TOKENS, BLOCK_TOKENS), 0)
        query_col = lax.broadcasted_iota(jnp.int32, (BLOCK_TOKENS, BLOCK_TOKENS), 1)
        causal = key_row <= query_col
    heads = [i * groups + g for g in range(groups) for i in range(kv_local)]
    scores, weights, rescales, ends = {}, {}, {}, {}

    def score(h):
        scores[h] = jnp.dot(keys[h // groups], qt_ref[qb, :, tile(h)], preferred_element_type=jnp.float32)

    def soften(h):
        whole = scores.pop(h)
        parts = [whole[tile(j)] * SCALE2 for j in range(blocks)]
        if first:
            parts[diagonal] = jnp.where(causal, parts[diagonal], -FAR)
        peak = functools.reduce(
            jnp.maximum, [jnp.max(part, axis=0, keepdims=True) - gap for part, gap in zip(parts, gaps)]
        )
        if not first:
            old_peak = ml_ref[place, 0:1, tile(h)]
            peak = jnp.maximum(peak, old_peak)
        exps = [jnp.exp2(part - (peak + gap)) for part, gap in zip(parts, gaps)]
        total = functools.reduce(jnp.add, [jnp.sum(e, axis=0, keepdims=True) for e in exps])
        if not first:
            rescales[h] = jnp.exp2(old_peak - peak)
            total = total + ml_ref[place, 1:2, tile(h)] * rescales[h]
        if finish:
            ends[h] = peak, total
        else:
            ml_ref[place, 0:1, tile(h)] = peak
            ml_ref[place, 1:2, tile(h)] = total
        weights[h] = jnp.concatenate([e.astype(jnp.bfloat16) for e in exps], axis=0)

    def weigh(h):
        weighted = jnp.dot(values[h // groups], weights.pop(h), preferred_element_type=jnp.float32)
        if not first:
            weighted = weighted + acc_ref[place, :, tile(h)] * rescales.pop(h)
        if finish:
            finish(h, *ends.pop(h), weighted)
        else:
            acc_ref[place, :, tile(h)] = weighted

    for t in range(len(heads) + 2):
        if t < len(heads):
            score(heads[t])
        if 1 <= t <= len(heads):
            soften(heads[t - 1])
        if t >= 2:
            weigh(heads[t - 2])


def split_shards(pieces, refs):
    shards, refs = [], list(refs)
    for count in pieces:
        if count == 2:
            shards.append((refs.pop(0), refs.pop(0)))
        else:
            shards.append(halves(refs.pop(0)))
    return shards, refs


def halves(shard_ref):
    rows = shard_ref.shape[0] // 2
    return shard_ref.at[0:rows, :], shard_ref.at[rows : 2 * rows, :]


def gap_rows(gaps_ref, blocks, qb, mask):
    total = gaps_ref.shape[0] // blocks
    first = qb * total + (lax.axis_index("ctx") ^ mask) * blocks
    gaps = [gaps_ref[first + j] for j in range(blocks)]
    return gaps, functools.reduce(jnp.minimum, gaps)[0, 0] < FAR


def attend_shards(masks, blocks, first, count, gaps_ref, shards, **rest):
    for m, shard in zip(masks, shards):

        def step(place, carry):
            qb = first + place
            gaps, some = gap_rows(gaps_ref, blocks, qb, m)

            @pl.when(some)
            def _():
                attend(shard, qb, place, gaps, None, **rest)

            return carry

        if count == 1:
            step(0, 0)
        else:
            lax.fori_loop(0, count, step, 0)


def pack_kernel(k_hbm, v_hbm, shard_ref, values_ref, v_buf, sems):
    rows, width = v_buf.shape
    values = pltpu.make_async_copy(v_hbm, v_buf, sems.at[0])
    keys = pltpu.make_async_copy(k_hbm, shard_ref.at[0:rows, :], sems.at[1])
    values.start()
    keys.start()
    values.wait()
    for j in range(rows // BLOCK_TOKENS):
        for i in range(width // HEAD_SIZE):
            turned = v_buf[tile(j), tile(i)].T
            shard_ref[tile(rows // BLOCK_TOKENS + j), tile(i)] = turned
            values_ref[tile(j), tile(i)] = turned
    keys.wait()


def gaps_kernel(blocks, order_hbm, live_hbm, gaps_ref, flags_ref, order_ref, live_ref, place_ref, sems):
    total, slots = order_ref.shape[0], live_ref.shape[1]
    pairs = [(order_hbm, order_ref), (live_hbm, live_ref)]
    copies = [pltpu.make_async_copy(source, target, sems.at[i]) for i, (source, target) in enumerate(pairs)]
    for copy in copies:
        copy.start()

    def clear(i, carry):
        flags_ref[i] = 0
        return carry

    def invert(b, carry):
        place_ref[order_ref[b]] = b
        return carry

    lax.fori_loop(0, blocks * total, clear, 0, unroll=8)
    copies[0].wait()
    lax.fori_loop(0, total, invert, 0, unroll=8)
    copies[1].wait()
    me = lax.axis_index("ctx")
    for qb in range(blocks):
        row = order_ref[me * blocks + qb]

        def mark(slot, carry):
            entry = live_ref[row, slot]
            spot = qb * total + place_ref[jnp.maximum(entry, 0)]
            flags_ref[jnp.where(entry >= 0, spot, blocks * total)] = 1
            return carry

        lax.fori_loop(0, slots, mark, 0, unroll=4)

    def spread(i, carry):
        gaps_ref[i] = jnp.full(gaps_ref.shape[1:], jnp.where(flags_ref[i] != 0, 0.0, FAR), jnp.float32)
        return carry

    lax.fori_loop(0, blocks * total, spread, 0, unroll=8)


def own_kernel(blocks, kv_local, groups, gaps_ref, q_ref, own_ref, qt_ref, ml_ref, acc_ref):
    for qb in range(blocks):
        for h in range(kv_local * groups):
            qt_ref[qb, :, tile(h)] = q_ref[tile(qb), tile(h)].T
        gaps, _ = gap_rows(gaps_ref, blocks, qb, 0)
        gaps[qb] = 0.0
        attend(halves(own_ref), qb, qb, gaps, qb, kv_local, groups, qt_ref, ml_ref, acc_ref)


def more_kernel(masks, pieces, blocks, kv_local, groups, gaps_ref, qt_ref, ml_in, acc_in, *refs):
    shards, (ml_ref, acc_ref) = split_shards(pieces, refs)
    ml_ref[...] = ml_in[...]
    acc_ref[...] = acc_in[...]
    attend_shards(
        masks, blocks, 0, blocks, gaps_ref, shards,
        kv_local=kv_local, groups=groups, qt_ref=qt_ref, ml_ref=ml_ref, acc_ref=acc_ref,
    )


def part_kernel(masks, pieces, blocks, part, step, cores, kv_local, groups, gaps_ref, qt_ref, ml_in, acc_in, *refs):
    shards, (ml_ref, acc_ref) = split_shards(pieces, refs)
    to = lax.rem(lax.axis_index("tp") + step, cores)
    for j in range(part):
        ml_ref[j] = ml_in[to * part + j]
        acc_ref[j] = acc_in[to * part + j]
    attend_shards(
        masks, blocks, to * part, part, gaps_ref, shards,
        kv_local=kv_local, groups=groups, qt_ref=qt_ref, ml_ref=ml_ref, acc_ref=acc_ref,
    )


def last_kernel(masks, pieces, blocks, part, step, cores, kv_local, groups, gaps_ref, qt_ref, ml_in, acc_in, *refs):
    shards, (out_ref, norm_ref, ml_ref, acc_ref) = split_shards(pieces, refs)
    to = lax.rem(lax.axis_index("tp") + step, cores)
    first = 0 if step else to * part
    for j in range(part):
        ml_ref[j] = ml_in[first + j]
        acc_ref[j] = acc_in[first + j]
    rest = dict(kv_local=kv_local, groups=groups, qt_ref=qt_ref, ml_ref=ml_ref, acc_ref=acc_ref)
    attend_shards(masks[:-1], blocks, to * part, part, gaps_ref, shards[:-1], **rest)
    for j in range(part):

        def finish(h, peak, denominator, weighted):
            normed = weighted * (1.0 / denominator)
            out_ref[tile(j), tile(h)] = normed.astype(jnp.bfloat16).T
            norm_ref[h : h + 1, tile(j)] = peak * LN2 + jnp.log(denominator)

        qb = to * part + j
        gaps, some = gap_rows(gaps_ref, blocks, qb, masks[-1])

        @pl.when(some)
        def _():
            attend(shards[-1], qb, j, gaps, None, finish=finish, **rest)

        @pl.when(jnp.logical_not(some))
        def _():
            for h in range(kv_local * groups):
                finish(h, ml_ref[j, 0:1, tile(h)], ml_ref[j, 1:2, tile(h)], acc_ref[j, :, tile(h)])


def place_kernel(cores, *refs):
    outs, norms, (out_hbm, norm_hbm, sems) = refs[:cores], refs[cores : 2 * cores], refs[2 * cores :]
    core = lax.axis_index("tp")
    copies = []
    for step in range(cores):
        origin = lax.rem(core + cores - step, cores)
        width = outs[step].shape[1]
        columns = pl.ds(pl.multiple_of(origin * width, HEAD_SIZE), width)
        copies.append(pltpu.make_async_copy(outs[step], out_hbm.at[:, columns], sems.at[step]))
    for step in range(cores):
        to = lax.rem(core + step, cores)
        width = norms[step].shape[1]
        columns = pl.ds(pl.multiple_of(to * width, BLOCK_TOKENS), width)
        copies.append(pltpu.make_async_copy(norms[step], norm_hbm.at[:, columns], sems.at[cores + step]))
    for copy in copies:
        copy.start()
    for copy in copies:
        copy.wait()


def body(queries, key_rows, value_rows, block_order, live_blocks):
    rows, width = queries.shape
    kv_local = key_rows.shape[1] // HEAD_SIZE
    heads = width // HEAD_SIZE
    groups = heads // kv_local
    blocks = rows // BLOCK_TOKENS
    shards = lax.axis_size("ctx")
    cores = lax.axis_size("tp")
    part = blocks // cores

    vmem = pl.BlockSpec(memory_space=pltpu.VMEM)
    hbm = pl.BlockSpec(memory_space=pltpu.HBM)
    qt_shape = jax.ShapeDtypeStruct((blocks, HEAD_SIZE, width), jnp.bfloat16)
    ml_shape = jax.ShapeDtypeStruct((blocks, 2, width), jnp.float32)
    acc_shape = jax.ShapeDtypeStruct((blocks, HEAD_SIZE, width), jnp.float32)

    def call(kernel, name, limit=VMEM_BYTES, **options):
        return pl.pallas_call(
            kernel,
            name=name,
            compiler_params=pltpu.CompilerParams(vmem_limit_bytes=limit),
            cost_estimate=pl.CostEstimate(flops=COST, bytes_accessed=COST, transcendentals=0),
            **options,
        )

    def in_hbm(array):
        return pltpu.with_memory_space_constraint(array, pltpu.HBM)

    def swap(array, distance):
        return lax.ppermute(array, "ctx", [(i, i ^ distance) for i in range(shards)])

    bits = [1 << i for i in range(shards.bit_length() - 1)]
    top = bits[-1]
    shard, values = call(
        pack_kernel,
        "pack",
        in_specs=[hbm] * 2,
        out_specs=[vmem] * 2,
        out_shape=[
            jax.ShapeDtypeStruct((2 * rows, kv_local * HEAD_SIZE), jnp.bfloat16),
            jax.ShapeDtypeStruct((rows, kv_local * HEAD_SIZE), jnp.bfloat16),
        ],
        scratch_shapes=[pltpu.VMEM(value_rows.shape, jnp.bfloat16), pltpu.SemaphoreType.DMA((2,))],
    )(in_hbm(key_rows), in_hbm(value_rows))
    gaps = call(
        functools.partial(gaps_kernel, blocks),
        "gaps",
        in_specs=[hbm] * 2,
        out_specs=vmem,
        out_shape=jax.ShapeDtypeStruct((blocks * block_order.shape[0], 1, BLOCK_TOKENS), jnp.float32),
        scratch_shapes=[
            pltpu.SMEM((blocks * block_order.shape[0] + 1,), jnp.int32),
            pltpu.SMEM(block_order.shape, jnp.int32),
            pltpu.SMEM(live_blocks.shape, jnp.int32),
            pltpu.SMEM(block_order.shape, jnp.int32),
            pltpu.SemaphoreType.DMA((2,)),
        ],
    )(in_hbm(block_order), in_hbm(live_blocks))
    got = {top: [swap(shard, top)]}
    for bit in reversed(bits[1:-1]):
        got[bit] = [swap(shard, bit)]
    got[1] = [swap(key_rows, 1), swap(values, 1)]

    qt, ml, acc = call(
        functools.partial(own_kernel, blocks, kv_local, groups),
        "own_shard",
        in_specs=[vmem] * 3,
        out_specs=[vmem] * 3,
        out_shape=[qt_shape, ml_shape, acc_shape],
    )(gaps, queries, shard)

    def more(masks, ml, acc):
        return call(
            functools.partial(more_kernel, masks, [len(got[m]) for m in masks], blocks, kv_local, groups),
            "more_shards",
            in_specs=[vmem] * (4 + sum(len(got[m]) for m in masks)),
            out_specs=[vmem] * 2,
            out_shape=[ml_shape, acc_shape],
        )(gaps, qt, ml, acc, *[array for m in masks for array in got[m]])

    def last(masks, step, ml, acc):
        arrays = [array for m in masks for array in got[m]]
        return call(
            functools.partial(
                last_kernel, masks, [len(got[m]) for m in masks], blocks, part, step, cores, kv_local, groups
            ),
            "last_shards",
            in_specs=[vmem] * (4 + len(arrays)),
            out_specs=[vmem, vmem],
            out_shape=[
                jax.ShapeDtypeStruct((part * BLOCK_TOKENS, width), jnp.bfloat16),
                jax.ShapeDtypeStruct((heads, part * BLOCK_TOKENS), jnp.float32),
            ],
            scratch_shapes=[
                pltpu.VMEM((part, *ml_shape.shape[1:]), jnp.float32),
                pltpu.VMEM((part, *acc_shape.shape[1:]), jnp.float32),
            ],
        )(gaps, qt, ml, acc, *arrays)

    def more_of_part(masks, step, ml, acc):
        arrays = [array for m in masks for array in got[m]]
        return call(
            functools.partial(
                part_kernel, masks, [len(got[m]) for m in masks], blocks, part, step, cores, kv_local, groups
            ),
            "part_shards",
            in_specs=[vmem] * (4 + len(arrays)),
            out_specs=[vmem] * 2,
            out_shape=[
                jax.ShapeDtypeStruct((part, *ml_shape.shape[1:]), jnp.float32),
                jax.ShapeDtypeStruct((part, *acc_shape.shape[1:]), jnp.float32),
            ],
        )(gaps, qt, ml, acc, *arrays)

    def after(arrays, *others):
        return [lax.optimization_barrier((array,) + others)[0] for array in arrays]

    several = sorted((m for m in range(shards) if m.bit_count() > 1), key=lambda m: (m.bit_count(), m))
    ml, acc = more([1], ml, acc)
    got[top] = after(got[top], acc)
    for bit in reversed(bits[1:-1]):
        got[bit] = after(got[bit], got[top][0])
        got[top] = after(got[top], got[bit][0])
    for m in several:
        if m & top and m.bit_count() == 2:
            got[m] = [swap(array, m & -m) for array in got[m & (m - 1)]]
    ml, acc = more(bits[1:], ml, acc)
    got[3] = [swap(jnp.concatenate(after(got[1], acc), axis=0), 2)]
    for m in several:
        if m not in got:
            got[m] = [swap(array, m & -m) for array in after(got[m & (m - 1)], acc)]
    final = [3, several[-1]]
    ready = [m for m in several if m not in final]
    for i in range(0, len(ready), CHUNK):
        ml, acc = more(ready[i : i + CHUNK], ml, acc)

    outs, norms = [None] * cores, [None] * cores
    for step in range(cores - 1, -1, -1):
        if step:
            outs[step], norms[step] = last(final[1:], step, *more_of_part(final[:1], step, ml, acc))
        else:
            outs[step], norms[step] = last(final, step, ml, acc)
        if step:
            outs[step] = lax.ppermute(outs[step], "tp", [(i, (i + step) % cores) for i in range(cores)])
    return call(
        functools.partial(place_kernel, cores),
        "place",
        in_specs=[vmem] * (2 * cores),
        out_specs=[hbm, hbm],
        out_shape=[
            jax.ShapeDtypeStruct((part * BLOCK_TOKENS, cores * width), jnp.bfloat16),
            jax.ShapeDtypeStruct((heads, rows), jnp.float32),
        ],
        scratch_shapes=[pltpu.SemaphoreType.DMA((2 * cores,))],
    )(*outs, *norms)


def solution(mesh):
    placed = (
        P(("rep", "ctx"), "tp"),
        P(("rep", "ctx"), "tp"),
        P(("rep", "ctx"), "tp"),
        P("rep"),
        P("rep", None),
    )
    return jax.shard_map(
        body,
        mesh=mesh,
        in_specs=placed,
        out_specs=(P(("rep", "ctx", "tp"), None), P(("rep", "tp"), "ctx")),
        check_vma=False,
    )
```

```python
import functools

import jax
import jax.numpy as jnp
import numpy as np
from jax import lax
from jax.experimental import pallas as pl
from jax.experimental.pallas import tpu as pltpu
from jax.sharding import PartitionSpec as P

HEAD_SIZE = 128
BLOCK_TOKENS = 128
SCALE2 = float(HEAD_SIZE**-0.5 * np.log2(np.e))
LN2 = float(np.log(2.0))
FAR = 1e30
VMEM_BYTES = 24 * 2**20
COST = 1024
CHUNK = 3


def tile(i):
    return slice(i * BLOCK_TOKENS, (i + 1) * BLOCK_TOKENS)


def attend(shard, qb, place, gaps, diagonal, kv_local, groups, qt_ref, ml_ref, acc_ref, finish=None):
    blocks = len(gaps)
    first = diagonal is not None
    keys_ref, values_ref = shard
    keys = [keys_ref[:, tile(i)] for i in range(kv_local)]
    values = [
        jnp.concatenate([values_ref[tile(j), tile(i)] for j in range(blocks)], axis=1) for i in range(kv_local)
    ]
    if first:
        key_row = lax.broadcasted_iota(jnp.int32, (BLOCK_TOKENS, BLOCK_TOKENS), 0)
        query_col = lax.broadcasted_iota(jnp.int32, (BLOCK_TOKENS, BLOCK_TOKENS), 1)
        causal = key_row <= query_col
    heads = [i * groups + g for g in range(groups) for i in range(kv_local)]
    scores, weights, rescales, ends = {}, {}, {}, {}

    def score(h):
        scores[h] = jnp.dot(keys[h // groups], qt_ref[qb, :, tile(h)], preferred_element_type=jnp.float32)

    def soften(h):
        whole = scores.pop(h)
        parts = [whole[tile(j)] * SCALE2 for j in range(blocks)]
        if first:
            parts[diagonal] = jnp.where(causal, parts[diagonal], -FAR)
        peak = functools.reduce(
            jnp.maximum, [jnp.max(part, axis=0, keepdims=True) - gap for part, gap in zip(parts, gaps)]
        )
        if not first:
            old_peak = ml_ref[place, 0:1, tile(h)]
            peak = jnp.maximum(peak, old_peak)
        exps = [jnp.exp2(part - (peak + gap)) for part, gap in zip(parts, gaps)]
        total = functools.reduce(jnp.add, [jnp.sum(e, axis=0, keepdims=True) for e in exps])
        if not first:
            rescales[h] = jnp.exp2(old_peak - peak)
            total = total + ml_ref[place, 1:2, tile(h)] * rescales[h]
        if finish:
            ends[h] = peak, total
        else:
            ml_ref[place, 0:1, tile(h)] = peak
            ml_ref[place, 1:2, tile(h)] = total
        weights[h] = jnp.concatenate([e.astype(jnp.bfloat16) for e in exps], axis=0)

    def weigh(h):
        weighted = jnp.dot(values[h // groups], weights.pop(h), preferred_element_type=jnp.float32)
        if not first:
            weighted = weighted + acc_ref[place, :, tile(h)] * rescales.pop(h)
        if finish:
            finish(h, *ends.pop(h), weighted)
        else:
            acc_ref[place, :, tile(h)] = weighted

    for t in range(len(heads) + 2):
        if t < len(heads):
            score(heads[t])
        if 1 <= t <= len(heads):
            soften(heads[t - 1])
        if t >= 2:
            weigh(heads[t - 2])


def split_shards(pieces, refs):
    shards, refs = [], list(refs)
    for count in pieces:
        if count == 2:
            shards.append((refs.pop(0), refs.pop(0)))
        else:
            shards.append(halves(refs.pop(0)))
    return shards, refs


def halves(shard_ref):
    rows = shard_ref.shape[0] // 2
    return shard_ref.at[0:rows, :], shard_ref.at[rows : 2 * rows, :]


def gap_rows(gaps_ref, blocks, qb, mask):
    total = gaps_ref.shape[0] // blocks
    first = qb * total + (lax.axis_index("ctx") ^ mask) * blocks
    gaps = [gaps_ref[first + j] for j in range(blocks)]
    return gaps, functools.reduce(jnp.minimum, gaps)[0, 0] < FAR


def attend_shards(masks, blocks, first, count, gaps_ref, shards, **rest):
    for m, shard in zip(masks, shards):

        def step(place, carry):
            qb = first + place
            gaps, some = gap_rows(gaps_ref, blocks, qb, m)

            @pl.when(some)
            def _():
                attend(shard, qb, place, gaps, None, **rest)

            return carry

        if count == 1:
            step(0, 0)
        else:
            lax.fori_loop(0, count, step, 0)


def pack_kernel(k_hbm, v_hbm, shard_ref, values_ref, v_buf, sems):
    rows, width = v_buf.shape
    values = pltpu.make_async_copy(v_hbm, v_buf, sems.at[0])
    keys = pltpu.make_async_copy(k_hbm, shard_ref.at[0:rows, :], sems.at[1])
    values.start()
    keys.start()
    values.wait()
    for j in range(rows // BLOCK_TOKENS):
        for i in range(width // HEAD_SIZE):
            turned = v_buf[tile(j), tile(i)].T
            shard_ref[tile(rows // BLOCK_TOKENS + j), tile(i)] = turned
            values_ref[tile(j), tile(i)] = turned
    keys.wait()


def gaps_kernel(blocks, order_hbm, live_hbm, gaps_ref, flags_ref, order_ref, live_ref, place_ref, sems):
    total, slots = order_ref.shape[0], live_ref.shape[1]
    pairs = [(order_hbm, order_ref), (live_hbm, live_ref)]
    copies = [pltpu.make_async_copy(source, target, sems.at[i]) for i, (source, target) in enumerate(pairs)]
    for copy in copies:
        copy.start()

    def clear(i, carry):
        flags_ref[i] = 0
        return carry

    def invert(b, carry):
        place_ref[order_ref[b]] = b
        return carry

    lax.fori_loop(0, blocks * total, clear, 0, unroll=8)
    copies[0].wait()
    lax.fori_loop(0, total, invert, 0, unroll=8)
    copies[1].wait()
    me = lax.axis_index("ctx")
    for qb in range(blocks):
        row = order_ref[me * blocks + qb]

        def mark(slot, carry):
            entry = live_ref[row, slot]
            spot = qb * total + place_ref[jnp.maximum(entry, 0)]
            flags_ref[jnp.where(entry >= 0, spot, blocks * total)] = 1
            return carry

        lax.fori_loop(0, slots, mark, 0, unroll=4)

    def spread(i, carry):
        gaps_ref[i] = jnp.full(gaps_ref.shape[1:], jnp.where(flags_ref[i] != 0, 0.0, FAR), jnp.float32)
        return carry

    lax.fori_loop(0, blocks * total, spread, 0, unroll=8)


def own_kernel(blocks, kv_local, groups, gaps_ref, q_ref, own_ref, qt_ref, ml_ref, acc_ref):
    for qb in range(blocks):
        for h in range(kv_local * groups):
            qt_ref[qb, :, tile(h)] = q_ref[tile(qb), tile(h)].T
        gaps, _ = gap_rows(gaps_ref, blocks, qb, 0)
        gaps[qb] = 0.0
        attend(halves(own_ref), qb, qb, gaps, qb, kv_local, groups, qt_ref, ml_ref, acc_ref)


def more_kernel(masks, pieces, blocks, kv_local, groups, gaps_ref, qt_ref, ml_in, acc_in, *refs):
    shards, (ml_ref, acc_ref) = split_shards(pieces, refs)
    ml_ref[...] = ml_in[...]
    acc_ref[...] = acc_in[...]
    attend_shards(
        masks, blocks, 0, blocks, gaps_ref, shards,
        kv_local=kv_local, groups=groups, qt_ref=qt_ref, ml_ref=ml_ref, acc_ref=acc_ref,
    )


def last_kernel(masks, pieces, blocks, part, step, cores, kv_local, groups, gaps_ref, qt_ref, ml_in, acc_in, *refs):
    shards, (out_ref, norm_ref, ml_ref, acc_ref) = split_shards(pieces, refs)
    to = lax.rem(lax.axis_index("tp") + step, cores)
    first = to * part
    for j in range(part):
        ml_ref[j] = ml_in[first + j]
        acc_ref[j] = acc_in[first + j]
    rest = dict(kv_local=kv_local, groups=groups, qt_ref=qt_ref, ml_ref=ml_ref, acc_ref=acc_ref)
    attend_shards(masks[:-1], blocks, to * part, part, gaps_ref, shards[:-1], **rest)
    for j in range(part):

        def finish(h, peak, denominator, weighted):
            normed = weighted * (1.0 / denominator)
            out_ref[tile(j), tile(h)] = normed.astype(jnp.bfloat16).T
            norm_ref[h : h + 1, tile(j)] = peak * LN2 + jnp.log(denominator)

        qb = to * part + j
        gaps, some = gap_rows(gaps_ref, blocks, qb, masks[-1])

        @pl.when(some)
        def _():
            attend(shards[-1], qb, j, gaps, None, finish=finish, **rest)

        @pl.when(jnp.logical_not(some))
        def _():
            for h in range(kv_local * groups):
                finish(h, ml_ref[j, 0:1, tile(h)], ml_ref[j, 1:2, tile(h)], acc_ref[j, :, tile(h)])


def place_kernel(cores, *refs):
    outs, norms, (out_hbm, norm_hbm, sems) = refs[:cores], refs[cores : 2 * cores], refs[2 * cores :]
    core = lax.axis_index("tp")
    copies = []
    for step in range(cores):
        origin = lax.rem(core + cores - step, cores)
        width = outs[step].shape[1]
        columns = pl.ds(pl.multiple_of(origin * width, HEAD_SIZE), width)
        copies.append(pltpu.make_async_copy(outs[step], out_hbm.at[:, columns], sems.at[step]))
    for step in range(cores):
        to = lax.rem(core + step, cores)
        width = norms[step].shape[1]
        columns = pl.ds(pl.multiple_of(to * width, BLOCK_TOKENS), width)
        copies.append(pltpu.make_async_copy(norms[step], norm_hbm.at[:, columns], sems.at[cores + step]))
    for copy in copies:
        copy.start()
    for copy in copies:
        copy.wait()


def body(queries, key_rows, value_rows, block_order, live_blocks):
    rows, width = queries.shape
    kv_local = key_rows.shape[1] // HEAD_SIZE
    heads = width // HEAD_SIZE
    groups = heads // kv_local
    blocks = rows // BLOCK_TOKENS
    shards = lax.axis_size("ctx")
    cores = lax.axis_size("tp")
    part = blocks // cores

    vmem = pl.BlockSpec(memory_space=pltpu.VMEM)
    hbm = pl.BlockSpec(memory_space=pltpu.HBM)
    qt_shape = jax.ShapeDtypeStruct((blocks, HEAD_SIZE, width), jnp.bfloat16)
    ml_shape = jax.ShapeDtypeStruct((blocks, 2, width), jnp.float32)
    acc_shape = jax.ShapeDtypeStruct((blocks, HEAD_SIZE, width), jnp.float32)

    def call(kernel, name, limit=VMEM_BYTES, **options):
        return pl.pallas_call(
            kernel,
            name=name,
            compiler_params=pltpu.CompilerParams(vmem_limit_bytes=limit),
            cost_estimate=pl.CostEstimate(flops=COST, bytes_accessed=COST, transcendentals=0),
            **options,
        )

    def in_hbm(array):
        return pltpu.with_memory_space_constraint(array, pltpu.HBM)

    def swap(array, distance):
        return lax.ppermute(array, "ctx", [(i, i ^ distance) for i in range(shards)])

    bits = [1 << i for i in range(shards.bit_length() - 1)]
    top = bits[-1]
    shard, values = call(
        pack_kernel,
        "pack",
        in_specs=[hbm] * 2,
        out_specs=[vmem] * 2,
        out_shape=[
            jax.ShapeDtypeStruct((2 * rows, kv_local * HEAD_SIZE), jnp.bfloat16),
            jax.ShapeDtypeStruct((rows, kv_local * HEAD_SIZE), jnp.bfloat16),
        ],
        scratch_shapes=[pltpu.VMEM(value_rows.shape, jnp.bfloat16), pltpu.SemaphoreType.DMA((2,))],
    )(in_hbm(key_rows), in_hbm(value_rows))
    gaps = call(
        functools.partial(gaps_kernel, blocks),
        "gaps",
        in_specs=[hbm] * 2,
        out_specs=vmem,
        out_shape=jax.ShapeDtypeStruct((blocks * block_order.shape[0], 1, BLOCK_TOKENS), jnp.float32),
        scratch_shapes=[
            pltpu.SMEM((blocks * block_order.shape[0] + 1,), jnp.int32),
            pltpu.SMEM(block_order.shape, jnp.int32),
            pltpu.SMEM(live_blocks.shape, jnp.int32),
            pltpu.SMEM(block_order.shape, jnp.int32),
            pltpu.SemaphoreType.DMA((2,)),
        ],
    )(in_hbm(block_order), in_hbm(live_blocks))
    got = {top: [swap(shard, top)]}
    for bit in reversed(bits[1:-1]):
        got[bit] = [swap(shard, bit)]
    got[1] = [swap(key_rows, 1), swap(values, 1)]

    qt, ml, acc = call(
        functools.partial(own_kernel, blocks, kv_local, groups),
        "own_shard",
        in_specs=[vmem] * 3,
        out_specs=[vmem] * 3,
        out_shape=[qt_shape, ml_shape, acc_shape],
    )(gaps, queries, shard)

    def more(masks, ml, acc):
        return call(
            functools.partial(more_kernel, masks, [len(got[m]) for m in masks], blocks, kv_local, groups),
            "more_shards",
            in_specs=[vmem] * (4 + sum(len(got[m]) for m in masks)),
            out_specs=[vmem] * 2,
            out_shape=[ml_shape, acc_shape],
        )(gaps, qt, ml, acc, *[array for m in masks for array in got[m]])

    def last(masks, step, ml, acc):
        arrays = [array for m in masks for array in got[m]]
        return call(
            functools.partial(
                last_kernel, masks, [len(got[m]) for m in masks], blocks, part, step, cores, kv_local, groups
            ),
            "last_shards",
            in_specs=[vmem] * (4 + len(arrays)),
            out_specs=[vmem, vmem],
            out_shape=[
                jax.ShapeDtypeStruct((part * BLOCK_TOKENS, width), jnp.bfloat16),
                jax.ShapeDtypeStruct((heads, part * BLOCK_TOKENS), jnp.float32),
            ],
            scratch_shapes=[
                pltpu.VMEM((part, *ml_shape.shape[1:]), jnp.float32),
                pltpu.VMEM((part, *acc_shape.shape[1:]), jnp.float32),
            ],
        )(gaps, qt, ml, acc, *arrays)

    def after(arrays, *others):
        return [lax.optimization_barrier((array,) + others)[0] for array in arrays]

    several = sorted((m for m in range(shards) if m.bit_count() > 1), key=lambda m: (m.bit_count(), m))
    ml, acc = more([1], ml, acc)
    got[top] = after(got[top], acc)
    for bit in reversed(bits[1:-1]):
        got[bit] = after(got[bit], got[top][0])
        got[top] = after(got[top], got[bit][0])
    for m in several:
        if m & top and m.bit_count() == 2:
            got[m] = [swap(array, m & -m) for array in got[m & (m - 1)]]
    ml, acc = more(bits[1:], ml, acc)
    got[3] = [swap(jnp.concatenate(after(got[1], acc), axis=0), 2)]
    for m in several:
        if m not in got:
            got[m] = [swap(array, m & -m) for array in after(got[m & (m - 1)], acc)]
    final = [3, several[-1]]
    ready = [m for m in several if m not in final]
    for i in range(0, len(ready), CHUNK):
        ml, acc = more(ready[i : i + CHUNK], ml, acc)
    ml, acc = more(final[:1], ml, acc)
    final = final[1:]

    outs, norms = [None] * cores, [None] * cores
    for step in range(cores - 1, -1, -1):
        outs[step], norms[step] = last(final, step, ml, acc)
        if step:
            outs[step] = lax.ppermute(outs[step], "tp", [(i, (i + step) % cores) for i in range(cores)])
    return call(
        functools.partial(place_kernel, cores),
        "place",
        in_specs=[vmem] * (2 * cores),
        out_specs=[hbm, hbm],
        out_shape=[
            jax.ShapeDtypeStruct((part * BLOCK_TOKENS, cores * width), jnp.bfloat16),
            jax.ShapeDtypeStruct((heads, rows), jnp.float32),
        ],
        scratch_shapes=[pltpu.SemaphoreType.DMA((2 * cores,))],
    )(*outs, *norms)


def solution(mesh):
    placed = (
        P(("rep", "ctx"), "tp"),
        P(("rep", "ctx"), "tp"),
        P(("rep", "ctx"), "tp"),
        P("rep"),
        P("rep", None),
    )
    return jax.shard_map(
        body,
        mesh=mesh,
        in_specs=placed,
        out_specs=(P(("rep", "ctx", "tp"), None), P(("rep", "tp"), "ctx")),
        check_vma=False,
    )
```

```python
import functools

import jax
import jax.numpy as jnp
import numpy as np
from jax import lax
from jax.experimental import pallas as pl
from jax.experimental.pallas import tpu as pltpu
from jax.sharding import PartitionSpec as P

HEAD_SIZE = 128
BLOCK_TOKENS = 128
SCALE2 = float(HEAD_SIZE**-0.5 * np.log2(np.e))
LN2 = float(np.log(2.0))
FAR = 1e30
VMEM_BYTES = 24 * 2**20
COST = 1024
CHUNK = 3


def tile(i):
    return slice(i * BLOCK_TOKENS, (i + 1) * BLOCK_TOKENS)


def attend(shard, qb, place, gaps, diagonal, kv_local, groups, qt_ref, ml_ref, acc_ref, finish=None):
    blocks = len(gaps)
    first = diagonal is not None
    keys_ref, values_ref = shard
    keys = [keys_ref[:, tile(i)] for i in range(kv_local)]
    values = [
        jnp.concatenate([values_ref[tile(j), tile(i)] for j in range(blocks)], axis=1) for i in range(kv_local)
    ]
    if first:
        key_row = lax.broadcasted_iota(jnp.int32, (BLOCK_TOKENS, BLOCK_TOKENS), 0)
        query_col = lax.broadcasted_iota(jnp.int32, (BLOCK_TOKENS, BLOCK_TOKENS), 1)
        causal = key_row <= query_col
    heads = [i * groups + g for g in range(groups) for i in range(kv_local)]
    scores, weights, rescales, ends = {}, {}, {}, {}

    def score(h):
        scores[h] = jnp.dot(keys[h // groups], qt_ref[qb, :, tile(h)], preferred_element_type=jnp.float32)

    def soften(h):
        whole = scores.pop(h)
        parts = [whole[tile(j)] * SCALE2 for j in range(blocks)]
        if first:
            parts[diagonal] = jnp.where(causal, parts[diagonal], -FAR)
        peak = functools.reduce(
            jnp.maximum, [jnp.max(part, axis=0, keepdims=True) - gap for part, gap in zip(parts, gaps)]
        )
        if not first:
            old_peak = ml_ref[place, 0:1, tile(h)]
            peak = jnp.maximum(peak, old_peak)
        exps = [jnp.exp2(part - (peak + gap)) for part, gap in zip(parts, gaps)]
        total = functools.reduce(jnp.add, [jnp.sum(e, axis=0, keepdims=True) for e in exps])
        if not first:
            rescales[h] = jnp.exp2(old_peak - peak)
            total = total + ml_ref[place, 1:2, tile(h)] * rescales[h]
        if finish:
            ends[h] = peak, total
        else:
            ml_ref[place, 0:1, tile(h)] = peak
            ml_ref[place, 1:2, tile(h)] = total
        weights[h] = jnp.concatenate([e.astype(jnp.bfloat16) for e in exps], axis=0)

    def weigh(h):
        weighted = jnp.dot(values[h // groups], weights.pop(h), preferred_element_type=jnp.float32)
        if not first:
            weighted = weighted + acc_ref[place, :, tile(h)] * rescales.pop(h)
        if finish:
            finish(h, *ends.pop(h), weighted)
        else:
            acc_ref[place, :, tile(h)] = weighted

    for t in range(len(heads) + 2):
        if t < len(heads):
            score(heads[t])
        if 1 <= t <= len(heads):
            soften(heads[t - 1])
        if t >= 2:
            weigh(heads[t - 2])


def split_shards(pieces, refs):
    shards, refs = [], list(refs)
    for count in pieces:
        if count == 2:
            shards.append((refs.pop(0), refs.pop(0)))
        else:
            shards.append(halves(refs.pop(0)))
    return shards, refs


def halves(shard_ref):
    rows = shard_ref.shape[0] // 2
    return shard_ref.at[0:rows, :], shard_ref.at[rows : 2 * rows, :]


def gap_rows(gaps_ref, blocks, qb, mask):
    total = gaps_ref.shape[0] // blocks
    first = qb * total + (lax.axis_index("ctx") ^ mask) * blocks
    gaps = [gaps_ref[first + j] for j in range(blocks)]
    return gaps, functools.reduce(jnp.minimum, gaps)[0, 0] < FAR


def attend_shards(masks, blocks, first, count, gaps_ref, shards, **rest):
    for m, shard in zip(masks, shards):

        def step(place, carry):
            qb = first + place
            gaps, some = gap_rows(gaps_ref, blocks, qb, m)

            @pl.when(some)
            def _():
                attend(shard, qb, place, gaps, None, **rest)

            return carry

        if count == 1:
            step(0, 0)
        else:
            lax.fori_loop(0, count, step, 0)


def pack_kernel(k_hbm, v_hbm, shard_ref, values_ref, v_buf, sems):
    rows, width = v_buf.shape
    values = pltpu.make_async_copy(v_hbm, v_buf, sems.at[0])
    keys = pltpu.make_async_copy(k_hbm, shard_ref.at[0:rows, :], sems.at[1])
    values.start()
    keys.start()
    values.wait()
    for j in range(rows // BLOCK_TOKENS):
        for i in range(width // HEAD_SIZE):
            turned = v_buf[tile(j), tile(i)].T
            shard_ref[tile(rows // BLOCK_TOKENS + j), tile(i)] = turned
            values_ref[tile(j), tile(i)] = turned
    keys.wait()


def gaps_kernel(blocks, order_hbm, live_hbm, gaps_ref, flags_ref, order_ref, live_ref, place_ref, sems):
    total, slots = order_ref.shape[0], live_ref.shape[1]
    pairs = [(order_hbm, order_ref), (live_hbm, live_ref)]
    copies = [pltpu.make_async_copy(source, target, sems.at[i]) for i, (source, target) in enumerate(pairs)]
    for copy in copies:
        copy.start()

    def clear(i, carry):
        flags_ref[i] = 0
        return carry

    def invert(b, carry):
        place_ref[order_ref[b]] = b
        return carry

    lax.fori_loop(0, blocks * total, clear, 0, unroll=8)
    copies[0].wait()
    lax.fori_loop(0, total, invert, 0, unroll=8)
    copies[1].wait()
    me = lax.axis_index("ctx")
    for qb in range(blocks):
        row = order_ref[me * blocks + qb]

        def mark(slot, carry):
            entry = live_ref[row, slot]
            spot = qb * total + place_ref[jnp.maximum(entry, 0)]
            flags_ref[jnp.where(entry >= 0, spot, blocks * total)] = 1
            return carry

        lax.fori_loop(0, slots, mark, 0, unroll=4)

    def spread(i, carry):
        gaps_ref[i] = jnp.full(gaps_ref.shape[1:], jnp.where(flags_ref[i] != 0, 0.0, FAR), jnp.float32)
        return carry

    lax.fori_loop(0, blocks * total, spread, 0, unroll=8)


def own_kernel(blocks, kv_local, groups, gaps_ref, q_ref, own_ref, qt_ref, ml_ref, acc_ref):
    for qb in range(blocks):
        for h in range(kv_local * groups):
            qt_ref[qb, :, tile(h)] = q_ref[tile(qb), tile(h)].T
        gaps, _ = gap_rows(gaps_ref, blocks, qb, 0)
        gaps[qb] = 0.0
        attend(halves(own_ref), qb, qb, gaps, qb, kv_local, groups, qt_ref, ml_ref, acc_ref)


def more_kernel(masks, pieces, blocks, kv_local, groups, gaps_ref, qt_ref, ml_in, acc_in, *refs):
    shards, (ml_ref, acc_ref) = split_shards(pieces, refs)
    ml_ref[...] = ml_in[...]
    acc_ref[...] = acc_in[...]
    attend_shards(
        masks, blocks, 0, blocks, gaps_ref, shards,
        kv_local=kv_local, groups=groups, qt_ref=qt_ref, ml_ref=ml_ref, acc_ref=acc_ref,
    )


def last_kernel(masks, pieces, blocks, part, step, cores, kv_local, groups, gaps_ref, qt_ref, ml_in, acc_in, *refs):
    shards, (out_ref, norm_ref, ml_ref, acc_ref) = split_shards(pieces, refs)
    to = lax.rem(lax.axis_index("tp") + step, cores)
    first = to * part
    for j in range(part):
        ml_ref[j] = ml_in[first + j]
        acc_ref[j] = acc_in[first + j]
    rest = dict(kv_local=kv_local, groups=groups, qt_ref=qt_ref, ml_ref=ml_ref, acc_ref=acc_ref)
    attend_shards(masks[:-1], blocks, to * part, part, gaps_ref, shards[:-1], **rest)
    for j in range(part):

        def finish(h, peak, denominator, weighted):
            normed = weighted * (1.0 / denominator)
            out_ref[tile(j), tile(h)] = normed.astype(jnp.bfloat16).T
            norm_ref[h : h + 1, tile(j)] = peak * LN2 + jnp.log(denominator)

        qb = to * part + j
        gaps, some = gap_rows(gaps_ref, blocks, qb, masks[-1])

        @pl.when(some)
        def _():
            attend(shards[-1], qb, j, gaps, None, finish=finish, **rest)

        @pl.when(jnp.logical_not(some))
        def _():
            for h in range(kv_local * groups):
                finish(h, ml_ref[j, 0:1, tile(h)], ml_ref[j, 1:2, tile(h)], acc_ref[j, :, tile(h)])


def place_kernel(cores, *refs):
    outs, norms, (out_hbm, norm_hbm, sems) = refs[:cores], refs[cores : 2 * cores], refs[2 * cores :]
    core = lax.axis_index("tp")
    copies = []
    for step in range(cores):
        origin = lax.rem(core + cores - step, cores)
        width = outs[step].shape[1]
        columns = pl.ds(pl.multiple_of(origin * width, HEAD_SIZE), width)
        copies.append(pltpu.make_async_copy(outs[step], out_hbm.at[:, columns], sems.at[step]))
    for step in range(cores):
        to = lax.rem(core + step, cores)
        width = norms[step].shape[1]
        columns = pl.ds(pl.multiple_of(to * width, BLOCK_TOKENS), width)
        copies.append(pltpu.make_async_copy(norms[step], norm_hbm.at[:, columns], sems.at[cores + step]))
    for copy in copies:
        copy.start()
    for copy in copies:
        copy.wait()


def body(queries, key_rows, value_rows, block_order, live_blocks):
    rows, width = queries.shape
    kv_local = key_rows.shape[1] // HEAD_SIZE
    heads = width // HEAD_SIZE
    groups = heads // kv_local
    blocks = rows // BLOCK_TOKENS
    shards = lax.axis_size("ctx")
    cores = lax.axis_size("tp")
    part = blocks // cores

    vmem = pl.BlockSpec(memory_space=pltpu.VMEM)
    hbm = pl.BlockSpec(memory_space=pltpu.HBM)
    qt_shape = jax.ShapeDtypeStruct((blocks, HEAD_SIZE, width), jnp.bfloat16)
    ml_shape = jax.ShapeDtypeStruct((blocks, 2, width), jnp.float32)
    acc_shape = jax.ShapeDtypeStruct((blocks, HEAD_SIZE, width), jnp.float32)

    def call(kernel, name, limit=VMEM_BYTES, **options):
        return pl.pallas_call(
            kernel,
            name=name,
            compiler_params=pltpu.CompilerParams(vmem_limit_bytes=limit),
            cost_estimate=pl.CostEstimate(flops=COST, bytes_accessed=COST, transcendentals=0),
            **options,
        )

    def in_hbm(array):
        return pltpu.with_memory_space_constraint(array, pltpu.HBM)

    def swap(array, distance):
        return lax.ppermute(array, "ctx", [(i, i ^ distance) for i in range(shards)])

    bits = [1 << i for i in range(shards.bit_length() - 1)]
    top = bits[-1]
    shard, values = call(
        pack_kernel,
        "pack",
        in_specs=[hbm] * 2,
        out_specs=[vmem] * 2,
        out_shape=[
            jax.ShapeDtypeStruct((2 * rows, kv_local * HEAD_SIZE), jnp.bfloat16),
            jax.ShapeDtypeStruct((rows, kv_local * HEAD_SIZE), jnp.bfloat16),
        ],
        scratch_shapes=[pltpu.VMEM(value_rows.shape, jnp.bfloat16), pltpu.SemaphoreType.DMA((2,))],
    )(in_hbm(key_rows), in_hbm(value_rows))
    gaps = call(
        functools.partial(gaps_kernel, blocks),
        "gaps",
        in_specs=[hbm] * 2,
        out_specs=vmem,
        out_shape=jax.ShapeDtypeStruct((blocks * block_order.shape[0], 1, BLOCK_TOKENS), jnp.float32),
        scratch_shapes=[
            pltpu.SMEM((blocks * block_order.shape[0] + 1,), jnp.int32),
            pltpu.SMEM(block_order.shape, jnp.int32),
            pltpu.SMEM(live_blocks.shape, jnp.int32),
            pltpu.SMEM(block_order.shape, jnp.int32),
            pltpu.SemaphoreType.DMA((2,)),
        ],
    )(in_hbm(block_order), in_hbm(live_blocks))
    got = {top: [swap(shard, top)]}
    for bit in reversed(bits[1:-1]):
        got[bit] = [swap(shard, bit)]
    got[1] = [swap(key_rows, 1), swap(values, 1)]

    qt, ml, acc = call(
        functools.partial(own_kernel, blocks, kv_local, groups),
        "own_shard",
        in_specs=[vmem] * 3,
        out_specs=[vmem] * 3,
        out_shape=[qt_shape, ml_shape, acc_shape],
    )(gaps, queries, shard)

    def more(masks, ml, acc):
        return call(
            functools.partial(more_kernel, masks, [len(got[m]) for m in masks], blocks, kv_local, groups),
            "more_shards",
            in_specs=[vmem] * (4 + sum(len(got[m]) for m in masks)),
            out_specs=[vmem] * 2,
            out_shape=[ml_shape, acc_shape],
        )(gaps, qt, ml, acc, *[array for m in masks for array in got[m]])

    def last(masks, step, ml, acc):
        arrays = [array for m in masks for array in got[m]]
        return call(
            functools.partial(
                last_kernel, masks, [len(got[m]) for m in masks], blocks, part, step, cores, kv_local, groups
            ),
            "last_shards",
            in_specs=[vmem] * (4 + len(arrays)),
            out_specs=[vmem, vmem],
            out_shape=[
                jax.ShapeDtypeStruct((part * BLOCK_TOKENS, width), jnp.bfloat16),
                jax.ShapeDtypeStruct((heads, part * BLOCK_TOKENS), jnp.float32),
            ],
            scratch_shapes=[
                pltpu.VMEM((part, *ml_shape.shape[1:]), jnp.float32),
                pltpu.VMEM((part, *acc_shape.shape[1:]), jnp.float32),
            ],
        )(gaps, qt, ml, acc, *arrays)

    def after(arrays, *others):
        return [lax.optimization_barrier((array,) + others)[0] for array in arrays]

    several = sorted((m for m in range(shards) if m.bit_count() > 1), key=lambda m: (m.bit_count(), m))
    ml, acc = more([1], ml, acc)
    got[top] = after(got[top], acc)
    for bit in reversed(bits[1:-1]):
        got[bit] = after(got[bit], got[top][0])
    for m in several:
        if m & top and m.bit_count() == 2:
            got[m] = [swap(array, m & -m) for array in got[m & (m - 1)]]
    ml, acc = more(bits[1:], ml, acc)
    got[3] = [swap(jnp.concatenate(after(got[1], acc), axis=0), 2)]
    for m in several:
        if m not in got:
            got[m] = [swap(array, m & -m) for array in after(got[m & (m - 1)], acc)]
    final = [3, several[-1]]
    ready = [m for m in several if m not in final]
    for i in range(0, len(ready), CHUNK):
        ml, acc = more(ready[i : i + CHUNK], ml, acc)
    ml, acc = more(final[:1], ml, acc)
    final = final[1:]

    outs, norms = [None] * cores, [None] * cores
    for step in range(cores - 1, -1, -1):
        outs[step], norms[step] = last(final, step, ml, acc)
        if step:
            outs[step] = lax.ppermute(outs[step], "tp", [(i, (i + step) % cores) for i in range(cores)])
    return call(
        functools.partial(place_kernel, cores),
        "place",
        in_specs=[vmem] * (2 * cores),
        out_specs=[hbm, hbm],
        out_shape=[
            jax.ShapeDtypeStruct((part * BLOCK_TOKENS, cores * width), jnp.bfloat16),
            jax.ShapeDtypeStruct((heads, rows), jnp.float32),
        ],
        scratch_shapes=[pltpu.SemaphoreType.DMA((2 * cores,))],
    )(*outs, *norms)


def solution(mesh):
    placed = (
        P(("rep", "ctx"), "tp"),
        P(("rep", "ctx"), "tp"),
        P(("rep", "ctx"), "tp"),
        P("rep"),
        P("rep", None),
    )
    return jax.shard_map(
        body,
        mesh=mesh,
        in_specs=placed,
        out_specs=(P(("rep", "ctx", "tp"), None), P(("rep", "tp"), "ctx")),
        check_vma=False,
    )
```

```python
import functools

import jax
import jax.numpy as jnp
import numpy as np
from jax import lax
from jax.experimental import pallas as pl
from jax.experimental.pallas import tpu as pltpu
from jax.sharding import PartitionSpec as P

HEAD_SIZE = 128
BLOCK_TOKENS = 128
SCALE2 = float(HEAD_SIZE**-0.5 * np.log2(np.e))
LN2 = float(np.log(2.0))
FAR = 1e30
VMEM_BYTES = 24 * 2**20
COST = 1024
CHUNK = 3


def tile(i):
    return slice(i * BLOCK_TOKENS, (i + 1) * BLOCK_TOKENS)


def attend(shard, qb, place, gaps, diagonal, kv_local, groups, qt_ref, ml_ref, acc_ref, finish=None):
    blocks = len(gaps)
    first = diagonal is not None
    keys_ref, values_ref = shard
    keys = [keys_ref[:, tile(i)] for i in range(kv_local)]
    values = [
        jnp.concatenate([values_ref[tile(j), tile(i)] for j in range(blocks)], axis=1) for i in range(kv_local)
    ]
    if first:
        key_row = lax.broadcasted_iota(jnp.int32, (BLOCK_TOKENS, BLOCK_TOKENS), 0)
        query_col = lax.broadcasted_iota(jnp.int32, (BLOCK_TOKENS, BLOCK_TOKENS), 1)
        causal = key_row <= query_col
    heads = [i * groups + g for g in range(groups) for i in range(kv_local)]
    scores, weights, rescales, ends = {}, {}, {}, {}

    def score(h):
        scores[h] = jnp.dot(keys[h // groups], qt_ref[qb, :, tile(h)], preferred_element_type=jnp.float32)

    def soften(h):
        whole = scores.pop(h)
        parts = [whole[tile(j)] for j in range(blocks)]
        if first:
            parts[diagonal] = jnp.where(causal, parts[diagonal], -FAR)
        peak = functools.reduce(
            jnp.maximum, [jnp.max(part, axis=0, keepdims=True) * SCALE2 - gap for part, gap in zip(parts, gaps)]
        )
        if not first:
            old_peak = ml_ref[place, 0:1, tile(h)]
            peak = jnp.maximum(peak, old_peak)
        exps = [jnp.exp2(part * SCALE2 - (peak + gap)) for part, gap in zip(parts, gaps)]
        total = functools.reduce(jnp.add, [jnp.sum(e, axis=0, keepdims=True) for e in exps])
        if not first:
            rescales[h] = jnp.exp2(old_peak - peak)
            total = total + ml_ref[place, 1:2, tile(h)] * rescales[h]
        if finish:
            ends[h] = peak, total
        else:
            ml_ref[place, 0:1, tile(h)] = peak
            ml_ref[place, 1:2, tile(h)] = total
        weights[h] = jnp.concatenate([e.astype(jnp.bfloat16) for e in exps], axis=0)

    def weigh(h):
        weighted = jnp.dot(values[h // groups], weights.pop(h), preferred_element_type=jnp.float32)
        if not first:
            weighted = weighted + acc_ref[place, :, tile(h)] * rescales.pop(h)
        if finish:
            finish(h, *ends.pop(h), weighted)
        else:
            acc_ref[place, :, tile(h)] = weighted

    for t in range(len(heads) + 2):
        if t < len(heads):
            score(heads[t])
        if 1 <= t <= len(heads):
            soften(heads[t - 1])
        if t >= 2:
            weigh(heads[t - 2])


def split_shards(pieces, refs):
    shards, refs = [], list(refs)
    for count in pieces:
        if count == 2:
            shards.append((refs.pop(0), refs.pop(0)))
        else:
            shards.append(halves(refs.pop(0)))
    return shards, refs


def halves(shard_ref):
    rows = shard_ref.shape[0] // 2
    return shard_ref.at[0:rows, :], shard_ref.at[rows : 2 * rows, :]


def gap_rows(gaps_ref, blocks, qb, mask):
    total = gaps_ref.shape[0] // blocks
    first = qb * total + (lax.axis_index("ctx") ^ mask) * blocks
    gaps = [gaps_ref[first + j] for j in range(blocks)]
    return gaps, functools.reduce(jnp.minimum, gaps)[0, 0] < FAR


def attend_shards(masks, blocks, first, count, gaps_ref, shards, **rest):
    for m, shard in zip(masks, shards):

        def step(place, carry):
            qb = first + place
            gaps, some = gap_rows(gaps_ref, blocks, qb, m)

            @pl.when(some)
            def _():
                attend(shard, qb, place, gaps, None, **rest)

            return carry

        if count == 1:
            step(0, 0)
        else:
            lax.fori_loop(0, count, step, 0)


def pack_kernel(k_hbm, v_hbm, shard_ref, values_ref, v_buf, sems):
    rows, width = v_buf.shape
    values = pltpu.make_async_copy(v_hbm, v_buf, sems.at[0])
    keys = pltpu.make_async_copy(k_hbm, shard_ref.at[0:rows, :], sems.at[1])
    values.start()
    keys.start()
    values.wait()
    for j in range(rows // BLOCK_TOKENS):
        for i in range(width // HEAD_SIZE):
            turned = v_buf[tile(j), tile(i)].T
            shard_ref[tile(rows // BLOCK_TOKENS + j), tile(i)] = turned
            values_ref[tile(j), tile(i)] = turned
    keys.wait()


def gaps_kernel(blocks, order_hbm, live_hbm, gaps_ref, flags_ref, order_ref, live_ref, place_ref, sems):
    total, slots = order_ref.shape[0], live_ref.shape[1]
    pairs = [(order_hbm, order_ref), (live_hbm, live_ref)]
    copies = [pltpu.make_async_copy(source, target, sems.at[i]) for i, (source, target) in enumerate(pairs)]
    for copy in copies:
        copy.start()

    def clear(i, carry):
        flags_ref[i] = 0
        return carry

    def invert(b, carry):
        place_ref[order_ref[b]] = b
        return carry

    lax.fori_loop(0, blocks * total, clear, 0, unroll=8)
    copies[0].wait()
    lax.fori_loop(0, total, invert, 0, unroll=8)
    copies[1].wait()
    me = lax.axis_index("ctx")
    for qb in range(blocks):
        row = order_ref[me * blocks + qb]

        def mark(slot, carry):
            entry = live_ref[row, slot]
            spot = qb * total + place_ref[jnp.maximum(entry, 0)]
            flags_ref[jnp.where(entry >= 0, spot, blocks * total)] = 1
            return carry

        lax.fori_loop(0, slots, mark, 0, unroll=4)

    def spread(i, carry):
        gaps_ref[i] = jnp.full(gaps_ref.shape[1:], jnp.where(flags_ref[i] != 0, 0.0, FAR), jnp.float32)
        return carry

    lax.fori_loop(0, blocks * total, spread, 0, unroll=8)


def own_kernel(blocks, kv_local, groups, gaps_ref, q_ref, own_ref, qt_ref, ml_ref, acc_ref):
    for qb in range(blocks):
        for h in range(kv_local * groups):
            qt_ref[qb, :, tile(h)] = q_ref[tile(qb), tile(h)].T
        gaps, _ = gap_rows(gaps_ref, blocks, qb, 0)
        gaps[qb] = 0.0
        attend(halves(own_ref), qb, qb, gaps, qb, kv_local, groups, qt_ref, ml_ref, acc_ref)


def more_kernel(masks, pieces, blocks, kv_local, groups, gaps_ref, qt_ref, ml_in, acc_in, *refs):
    shards, (ml_ref, acc_ref) = split_shards(pieces, refs)
    ml_ref[...] = ml_in[...]
    acc_ref[...] = acc_in[...]
    attend_shards(
        masks, blocks, 0, blocks, gaps_ref, shards,
        kv_local=kv_local, groups=groups, qt_ref=qt_ref, ml_ref=ml_ref, acc_ref=acc_ref,
    )


def last_kernel(masks, pieces, blocks, part, step, cores, kv_local, groups, gaps_ref, qt_ref, ml_in, acc_in, *refs):
    shards, (out_ref, norm_ref, ml_ref, acc_ref) = split_shards(pieces, refs)
    to = lax.rem(lax.axis_index("tp") + step, cores)
    first = to * part
    for j in range(part):
        ml_ref[j] = ml_in[first + j]
        acc_ref[j] = acc_in[first + j]
    rest = dict(kv_local=kv_local, groups=groups, qt_ref=qt_ref, ml_ref=ml_ref, acc_ref=acc_ref)
    attend_shards(masks[:-1], blocks, to * part, part, gaps_ref, shards[:-1], **rest)
    for j in range(part):

        def finish(h, peak, denominator, weighted):
            normed = weighted * (1.0 / denominator)
            out_ref[tile(j), tile(h)] = normed.astype(jnp.bfloat16).T
            norm_ref[h : h + 1, tile(j)] = peak * LN2 + jnp.log(denominator)

        qb = to * part + j
        gaps, some = gap_rows(gaps_ref, blocks, qb, masks[-1])

        @pl.when(some)
        def _():
            attend(shards[-1], qb, j, gaps, None, finish=finish, **rest)

        @pl.when(jnp.logical_not(some))
        def _():
            for h in range(kv_local * groups):
                finish(h, ml_ref[j, 0:1, tile(h)], ml_ref[j, 1:2, tile(h)], acc_ref[j, :, tile(h)])


def place_kernel(cores, *refs):
    outs, norms, (out_hbm, norm_hbm, sems) = refs[:cores], refs[cores : 2 * cores], refs[2 * cores :]
    core = lax.axis_index("tp")
    copies = []
    for step in range(cores):
        origin = lax.rem(core + cores - step, cores)
        width = outs[step].shape[1]
        columns = pl.ds(pl.multiple_of(origin * width, HEAD_SIZE), width)
        copies.append(pltpu.make_async_copy(outs[step], out_hbm.at[:, columns], sems.at[step]))
    for step in range(cores):
        to = lax.rem(core + step, cores)
        width = norms[step].shape[1]
        columns = pl.ds(pl.multiple_of(to * width, BLOCK_TOKENS), width)
        copies.append(pltpu.make_async_copy(norms[step], norm_hbm.at[:, columns], sems.at[cores + step]))
    for copy in copies:
        copy.start()
    for copy in copies:
        copy.wait()


def body(queries, key_rows, value_rows, block_order, live_blocks):
    rows, width = queries.shape
    kv_local = key_rows.shape[1] // HEAD_SIZE
    heads = width // HEAD_SIZE
    groups = heads // kv_local
    blocks = rows // BLOCK_TOKENS
    shards = lax.axis_size("ctx")
    cores = lax.axis_size("tp")
    part = blocks // cores

    vmem = pl.BlockSpec(memory_space=pltpu.VMEM)
    hbm = pl.BlockSpec(memory_space=pltpu.HBM)
    qt_shape = jax.ShapeDtypeStruct((blocks, HEAD_SIZE, width), jnp.bfloat16)
    ml_shape = jax.ShapeDtypeStruct((blocks, 2, width), jnp.float32)
    acc_shape = jax.ShapeDtypeStruct((blocks, HEAD_SIZE, width), jnp.float32)

    def call(kernel, name, limit=VMEM_BYTES, **options):
        return pl.pallas_call(
            kernel,
            name=name,
            compiler_params=pltpu.CompilerParams(vmem_limit_bytes=limit),
            cost_estimate=pl.CostEstimate(flops=COST, bytes_accessed=COST, transcendentals=0),
            **options,
        )

    def in_hbm(array):
        return pltpu.with_memory_space_constraint(array, pltpu.HBM)

    def swap(array, distance):
        return lax.ppermute(array, "ctx", [(i, i ^ distance) for i in range(shards)])

    bits = [1 << i for i in range(shards.bit_length() - 1)]
    top = bits[-1]
    shard, values = call(
        pack_kernel,
        "pack",
        in_specs=[hbm] * 2,
        out_specs=[vmem] * 2,
        out_shape=[
            jax.ShapeDtypeStruct((2 * rows, kv_local * HEAD_SIZE), jnp.bfloat16),
            jax.ShapeDtypeStruct((rows, kv_local * HEAD_SIZE), jnp.bfloat16),
        ],
        scratch_shapes=[pltpu.VMEM(value_rows.shape, jnp.bfloat16), pltpu.SemaphoreType.DMA((2,))],
    )(in_hbm(key_rows), in_hbm(value_rows))
    gaps = call(
        functools.partial(gaps_kernel, blocks),
        "gaps",
        in_specs=[hbm] * 2,
        out_specs=vmem,
        out_shape=jax.ShapeDtypeStruct((blocks * block_order.shape[0], 1, BLOCK_TOKENS), jnp.float32),
        scratch_shapes=[
            pltpu.SMEM((blocks * block_order.shape[0] + 1,), jnp.int32),
            pltpu.SMEM(block_order.shape, jnp.int32),
            pltpu.SMEM(live_blocks.shape, jnp.int32),
            pltpu.SMEM(block_order.shape, jnp.int32),
            pltpu.SemaphoreType.DMA((2,)),
        ],
    )(in_hbm(block_order), in_hbm(live_blocks))
    got = {top: [swap(shard, top)]}
    for bit in reversed(bits[1:-1]):
        got[bit] = [swap(shard, bit)]
    got[1] = [swap(key_rows, 1), swap(values, 1)]

    qt, ml, acc = call(
        functools.partial(own_kernel, blocks, kv_local, groups),
        "own_shard",
        in_specs=[vmem] * 3,
        out_specs=[vmem] * 3,
        out_shape=[qt_shape, ml_shape, acc_shape],
    )(gaps, queries, shard)

    def more(masks, ml, acc):
        return call(
            functools.partial(more_kernel, masks, [len(got[m]) for m in masks], blocks, kv_local, groups),
            "more_shards",
            in_specs=[vmem] * (4 + sum(len(got[m]) for m in masks)),
            out_specs=[vmem] * 2,
            out_shape=[ml_shape, acc_shape],
        )(gaps, qt, ml, acc, *[array for m in masks for array in got[m]])

    def last(masks, step, ml, acc):
        arrays = [array for m in masks for array in got[m]]
        return call(
            functools.partial(
                last_kernel, masks, [len(got[m]) for m in masks], blocks, part, step, cores, kv_local, groups
            ),
            "last_shards",
            in_specs=[vmem] * (4 + len(arrays)),
            out_specs=[vmem, vmem],
            out_shape=[
                jax.ShapeDtypeStruct((part * BLOCK_TOKENS, width), jnp.bfloat16),
                jax.ShapeDtypeStruct((heads, part * BLOCK_TOKENS), jnp.float32),
            ],
            scratch_shapes=[
                pltpu.VMEM((part, *ml_shape.shape[1:]), jnp.float32),
                pltpu.VMEM((part, *acc_shape.shape[1:]), jnp.float32),
            ],
        )(gaps, qt, ml, acc, *arrays)

    def after(arrays, *others):
        return [lax.optimization_barrier((array,) + others)[0] for array in arrays]

    several = sorted((m for m in range(shards) if m.bit_count() > 1), key=lambda m: (m.bit_count(), m))
    ml, acc = more([1], ml, acc)
    got[top] = after(got[top], acc)
    for bit in reversed(bits[1:-1]):
        got[bit] = after(got[bit], got[top][0])
    for m in several:
        if m & top and m.bit_count() == 2:
            got[m] = [swap(array, m & -m) for array in got[m & (m - 1)]]
    ml, acc = more(bits[1:], ml, acc)
    got[3] = [swap(jnp.concatenate(after(got[1], acc), axis=0), 2)]
    for m in several:
        if m not in got:
            got[m] = [swap(array, m & -m) for array in after(got[m & (m - 1)], acc)]
    final = [3, several[-1]]
    ready = [m for m in several if m not in final]
    for i in range(0, len(ready), CHUNK):
        ml, acc = more(ready[i : i + CHUNK], ml, acc)
    ml, acc = more(final[:1], ml, acc)
    final = final[1:]

    outs, norms = [None] * cores, [None] * cores
    for step in range(cores - 1, -1, -1):
        outs[step], norms[step] = last(final, step, ml, acc)
        if step:
            outs[step] = lax.ppermute(outs[step], "tp", [(i, (i + step) % cores) for i in range(cores)])
    return call(
        functools.partial(place_kernel, cores),
        "place",
        in_specs=[vmem] * (2 * cores),
        out_specs=[hbm, hbm],
        out_shape=[
            jax.ShapeDtypeStruct((part * BLOCK_TOKENS, cores * width), jnp.bfloat16),
            jax.ShapeDtypeStruct((heads, rows), jnp.float32),
        ],
        scratch_shapes=[pltpu.SemaphoreType.DMA((2 * cores,))],
    )(*outs, *norms)


def solution(mesh):
    placed = (
        P(("rep", "ctx"), "tp"),
        P(("rep", "ctx"), "tp"),
        P(("rep", "ctx"), "tp"),
        P("rep"),
        P("rep", None),
    )
    return jax.shard_map(
        body,
        mesh=mesh,
        in_specs=placed,
        out_specs=(P(("rep", "ctx", "tp"), None), P(("rep", "tp"), "ctx")),
        check_vma=False,
    )
```
